256 devices in a mesh: grp: 4 (over x), own: 64 (over y, z, core).
Axes of the slice: x: 4, y: 4, z: 8, core: 2. Of those that a mesh axis runs over, the one named last changes fastest.
Arguments:
- head_rows: bfloat16 [196608, 400], P(('grp', 'own'))
- tail_rows: bfloat16 [196608, 400], P(('grp', 'own'))
- rel_ids: int32 [196608], P(('grp', 'own')), may hold values from 0 to 1499
- neg_rows: bfloat16 [65536, 400], P(('grp', 'own'))
- rel_table: float32 [1500, 400], replicated
- owner_counts: int32 [256, 64], P(('grp', 'own')), may hold values from 1 to 16, as said below
- unique_ids: int32 [256, 1024], P(('grp', 'own')), may hold values from 0 to 1023, as said below
- head_slot: int32 [196608], P(('grp', 'own')), may hold values from 0 to 1023, as said below
- tail_slot: int32 [196608], P(('grp', 'own')), may hold values from 0 to 1023, as said below
- negative_slot: int32 [65536], P(('grp', 'own')), may hold values from 0 to 1023, as said below
Outputs:
- entity_grad: float32 [65536, 400], P('own', 'grp')
- rel_grad: float32 [1500, 400], replicated
The draws below stay inside these ranges and needn't reach their ends.
Inputs may be any that keep to these rules, and one draw needn't show every extreme that they name: `owner_counts`: every device's counts lie in 1 to 16; in every draw some partition receives exactly 16 entities from every device, and some device has all its counts equal to 16. `unique_ids`: within one device's list, the entries of one partition are distinct; entries past the sum of the device's counts are unused. `head_slot`: every slot points below the sum of its device's counts, and every such slot of a device is named by some head, tail or negative slot of that device. `tail_slot`: as for head_slot. `negative_slot`: as for head_slot.
All inputs are finite; a program needn't handle non-finite values.
Results may differ from the reference program's by a relative error of at most 0.0039.
Values may be sent and summed in bfloat16 or wider, within the bound.
No kernel may reach another device: no remote copies, remote signals or barrier semaphores. Data moves between devices by JAX's collectives and lax.ppermute only.
A program may use at most 64 MiB of HBM per device.

```python
import math
import jax
import jax.numpy as jnp
import numpy as np
from jax import lax

D = 400
RELS = 1500
E_DEV = 768
ENT_DEV = 1024
NEGATIVES_PER_GPU = 256
CAP = 16
EDGES = 196608
NEG = 1024
NEG_ALL = 65536
U_CAP = 1024
ENTITIES = 65536
N_GRP = 4
N_OWN = 64
DEVICES = 256


def negative_base(key):
    values = jax.random.normal(jax.random.fold_in(key, 21), (NEG_ALL, D), jnp.float32) * 0.25
    return jnp.clip(values, -1.5, 1.5)


def entity_rows(key, stride):
    key = jax.random.fold_in(key, stride)
    rows = jnp.clip(jax.random.normal(key, (EDGES, D), jnp.float32) * 0.25, -1.5, 1.5)
    return rows.astype(jnp.bfloat16)


def draw_head_rows(key, part):
    return entity_rows(key, 37)


def draw_tail_rows(key, part):
    return entity_rows(key, 53)


def draw_neg_rows(key, part):
    negatives = negative_base(key)
    return negatives.astype(jnp.bfloat16)


def draw_rel_table(key, part):
    key = jax.random.fold_in(key, 9)
    key_re, key_im = jax.random.split(key)
    real_part = jax.random.uniform(key_re, (RELS, D // 2), jnp.float32, 0.5, 1.5)
    imag_part = jax.random.uniform(key_im, (RELS, D // 2), jnp.float32, -0.5, 0.5)
    return jnp.concatenate([real_part, imag_part], -1)


def unique_plan(key):
    key_base = jax.random.fold_in(key, 11)
    key_hot = jax.random.fold_in(key, 12)
    key_offset = jax.random.fold_in(key, 13)
    key_filler = jax.random.fold_in(key, 14)
    key_perm = jax.random.fold_in(key, 15)
    key_full = jax.random.fold_in(key, 16)
    base_counts = jax.random.randint(key_base, (DEVICES, N_OWN), max(1, CAP // 5), CAP * 3 // 4 + 1)
    hot_owner = jax.random.randint(key_hot, (2,), 0, N_OWN)
    full_device = jax.random.randint(key_full, (), 0, DEVICES)
    lanes = jnp.arange(N_OWN, dtype=jnp.int32)
    is_hot = (lanes == hot_owner[0]) | (lanes == hot_owner[1])
    is_full = jnp.arange(DEVICES, dtype=jnp.int32) == full_device
    counts = jnp.where(is_hot[None, :] | is_full[:, None], CAP, base_counts).astype(jnp.int32)
    ends = jnp.cumsum(counts, 1).astype(jnp.int32)
    starts = ends - counts
    totals = ends[:, -1]
    position = jnp.arange(U_CAP, dtype=jnp.int32)
    partition = jnp.sum((position[None, :, None] >= ends[:, None, :]).astype(jnp.int32), -1)
    clamped = jnp.minimum(partition, N_OWN - 1)
    start_at = jnp.take_along_axis(starts, clamped, 1)
    offsets = jax.random.randint(key_offset, (DEVICES, N_OWN), 0, ENT_DEV)
    offset_at = jnp.take_along_axis(offsets, clamped, 1)
    local_rows = (offset_at + position[None, :] - start_at) % ENT_DEV
    filler = jax.random.randint(key_filler, (DEVICES, U_CAP), 0, ENT_DEV)
    uids = jnp.where(partition < N_OWN, local_rows, filler).astype(jnp.int32)
    row_count = 2 * E_DEV + NEGATIVES_PER_GPU
    perms = jax.vmap(lambda single: jax.random.permutation(single, row_count))(jax.random.split(key_perm, DEVICES))
    slot_entries = (perms % totals[:, None]).astype(jnp.int32)
    return (counts, uids, slot_entries)


def draw_owner_counts(key, part):
    return unique_plan(key)[0]


def draw_unique_ids(key, part):
    return unique_plan(key)[1]


def draw_head_slot(key, part):
    return unique_plan(key)[2][:, :E_DEV].reshape(EDGES)


def draw_tail_slot(key, part):
    return unique_plan(key)[2][:, E_DEV:2 * E_DEV].reshape(EDGES)


def draw_negative_slot(key, part):
    return unique_plan(key)[2][:, 2 * E_DEV:].reshape(NEG_ALL)


def set_ends(result, stream_key, smallest, top_value):
    index_at = [jax.random.randint(jax.random.fold_in(stream_key, axis), (), 0, length) for axis, length in enumerate(result.shape)]
    longest = result.shape.index(max(result.shape))
    neighbour = index_at[:longest] + [(index_at[longest] + 1) % result.shape[longest]] + index_at[longest + 1:]
    return result.at[tuple(index_at)].set(smallest).at[tuple(neighbour)].set(top_value)


def rank_bounds(count, slope):
    weights = [(1 << 20) // math.isqrt(grade ** slope) + 1 for grade in range(1, count + 1)]
    deviation = 1 + sum(weights) // (1 << 30)
    return np.cumsum(np.array([max(1, weight // deviation) for weight in weights]))


def ranked_ids(rng, shape, count, lean):
    table = rank_bounds(count, lean)
    pick = jax.random.randint(jax.random.fold_in(rng, 1), shape, 0, int(table[count - 1]))
    rank = jnp.searchsorted(jnp.asarray(table, jnp.int32), pick, side="right")
    return jax.random.permutation(jax.random.fold_in(rng, 2), count)[rank].astype(jnp.int32)


def setup_inputs(seed: int = 0) -> dict:
    arg_keys = jax.random.split(jax.random.key(seed), 11)
    return {
        "head_rows": draw_head_rows(jax.random.fold_in(arg_keys[10], 71), 0),
        "tail_rows": draw_tail_rows(jax.random.fold_in(arg_keys[10], 71), 0),
        "rel_ids": set_ends(ranked_ids(arg_keys[2], (EDGES,), RELS, 2), jax.random.fold_in(arg_keys[2], 3), 0, RELS - 1).astype(jnp.int32),
        "neg_rows": draw_neg_rows(jax.random.fold_in(arg_keys[10], 71), 0),
        "rel_table": draw_rel_table(jax.random.fold_in(arg_keys[10], 71), 0),
        "owner_counts": draw_owner_counts(jax.random.fold_in(arg_keys[10], 71), 0),
        "unique_ids": draw_unique_ids(jax.random.fold_in(arg_keys[10], 71), 0),
        "head_slot": draw_head_slot(jax.random.fold_in(arg_keys[10], 71), 0),
        "tail_slot": draw_tail_slot(jax.random.fold_in(arg_keys[10], 71), 0),
        "negative_slot": draw_negative_slot(jax.random.fold_in(arg_keys[10], 71), 0),
    }


def complex_mul(left, right):
    half_width = left.shape[-1] // 2
    left_re, left_im = left[..., :half_width], left[..., half_width:]
    right_re, right_im = right[..., :half_width], right[..., half_width:]
    return jnp.concatenate([left_re * right_re - left_im * right_im, left_re * right_im + left_im * right_re], -1)


def conjugate(value):
    half_width = value.shape[-1] // 2
    return jnp.concatenate([value[..., :half_width], -value[..., half_width:]], -1)


def one_side(query_rows, positive_rows, negatives):
    positive = jnp.sum(query_rows.astype(jnp.float32) * positive_rows.astype(jnp.float32), -1)
    scores = jnp.dot(query_rows, negatives.T, preferred_element_type=jnp.float32)
    top_score = jnp.maximum(positive, jnp.max(scores, -1))
    pos_weight = jnp.exp(positive - top_score)
    neg_weight = jnp.exp(scores - top_score[:, None])
    denominator = pos_weight + jnp.sum(neg_weight, -1)
    first_term = pos_weight / denominator - 1.0
    probs_bf = (neg_weight / denominator[:, None]).astype(jnp.bfloat16)
    return first_term, probs_bf


def local_grads(heads, tails, relations, negatives):
    head_f = heads.astype(jnp.float32)
    tail_f = tails.astype(jnp.float32)
    query = complex_mul(head_f, relations).astype(jnp.bfloat16)
    mirror = complex_mul(conjugate(relations), tail_f).astype(jnp.bfloat16)
    first_tail, probs_tail = one_side(query, tails, negatives)
    first_head, probs_head = one_side(mirror, heads, negatives)
    d_query = first_tail[:, None] * tail_f + jnp.dot(probs_tail, negatives, preferred_element_type=jnp.float32)
    d_mirror = first_head[:, None] * head_f + jnp.dot(probs_head, negatives, preferred_element_type=jnp.float32)
    d_heads = first_head[:, None] * mirror.astype(jnp.float32) + complex_mul(conjugate(relations), d_query)
    d_tails = first_tail[:, None] * query.astype(jnp.float32) + complex_mul(relations, d_mirror)
    d_rel = complex_mul(conjugate(head_f), d_query) + complex_mul(tail_f, conjugate(d_mirror))
    d_group = jnp.dot(probs_tail.T, query, preferred_element_type=jnp.float32) + jnp.dot(probs_head.T, mirror, preferred_element_type=jnp.float32)
    return d_heads, d_tails, d_rel, d_group


def reference(head_rows, tail_rows, rel_ids, neg_rows, rel_table, owner_counts, unique_ids, head_slot, tail_slot, negative_slot):
    heads_all = head_rows.reshape(N_GRP, N_OWN, E_DEV, D)
    tails_all = tail_rows.reshape(N_GRP, N_OWN, E_DEV, D)
    rels_all = rel_ids.reshape(N_GRP, N_OWN, E_DEV)
    negs_all = neg_rows.reshape(N_GRP, N_OWN, NEGATIVES_PER_GPU, D)
    head_slot_list = head_slot.reshape(N_GRP, N_OWN, E_DEV)
    tail_slot_list = tail_slot.reshape(N_GRP, N_OWN, E_DEV)
    negative_slot_list = negative_slot.reshape(N_GRP, N_OWN, NEGATIVES_PER_GPU)
    counts_all = owner_counts.reshape(N_GRP, N_OWN, N_OWN)
    uids_all = unique_ids.reshape(N_GRP, N_OWN, U_CAP)
    position = jnp.arange(U_CAP, dtype=jnp.int32)

    def group_step(carry, owner_device_index):
        ent_acc, rel_acc = carry
        negatives = negs_all[:, owner_device_index].reshape(NEG, D)
        results = []
        neg_total = jnp.zeros((NEG, D), jnp.float32)
        for member_entity in range(N_GRP):
            relations = jnp.take(rel_table, rels_all[member_entity, owner_device_index], axis=0)
            pieces = local_grads(heads_all[member_entity, owner_device_index], tails_all[member_entity, owner_device_index], relations, negatives)
            results.append(pieces)
            neg_total = neg_total + pieces[3]
        neg_split = neg_total.reshape(N_GRP, NEGATIVES_PER_GPU, D)
        for member_entity in range(N_GRP):
            d_heads, d_tails, d_rel, unused_group = results[member_entity]
            rows = jnp.concatenate([d_heads, d_tails, neg_split[member_entity]], 0)
            slot_entries = jnp.concatenate([head_slot_list[member_entity, owner_device_index], tail_slot_list[member_entity, owner_device_index], negative_slot_list[member_entity, owner_device_index]], 0).astype(jnp.int32)
            slot_sum = jax.ops.segment_sum(rows, slot_entries, num_segments=U_CAP)
            ends = jnp.cumsum(counts_all[member_entity, owner_device_index]).astype(jnp.int32)
            partition = jnp.sum((position[:, None] >= ends[None, :]).astype(jnp.int32), 1).astype(jnp.int32)
            target = jnp.where(partition < N_OWN, partition * ENT_DEV + uids_all[member_entity, owner_device_index], ENTITIES).astype(jnp.int32)
            ent_acc = ent_acc.at[target].add(slot_sum, mode="drop")
            rel_acc = rel_acc + jax.ops.segment_sum(d_rel, rels_all[member_entity, owner_device_index], num_segments=RELS)
        return (ent_acc, rel_acc), None

    start = (jnp.zeros((ENTITIES, D), jnp.float32), jnp.zeros((RELS, D), jnp.float32))
    (entity_grad, rel_grad), unused = lax.scan(group_step, start, jnp.arange(N_OWN, dtype=jnp.int32))
    return entity_grad, rel_grad
```

```python
import jax
import jax.numpy as jnp
from jax import lax
from jax.experimental import pallas as pl
from jax.experimental.pallas import tpu as pltpu
from jax.sharding import Mesh
from jax.sharding import PartitionSpec as P

D = 400
RELS = 1500
E_DEV = 768
ENT_DEV = 1024
NEG_DEV = 256
CAP = 16
NEG = 1024
U_CAP = 1024
N_GRP = 4
N_OWN = 64
N_YZ = 32
LANES = 128
USED = 100
W = N_GRP * LANES
HALF = W // 2
REL_PAD = 1536
REL_HALF = REL_PAD // 2
BLK = 256
ROWS = 2 * E_DEV
ALL = ("x", "y", "z", "c")
F32 = jnp.float32
BF16 = jnp.bfloat16
I32 = jnp.int32
VMEM_BYTES = 48 * 1024 * 1024


def dot(a, b):
    return lax.dot_general(a, b, (((1,), (0,)), ((), ())), preferred_element_type=F32)


def dot_nt(a, b):
    return lax.dot_general(a, b, (((1,), (1,)), ((), ())), preferred_element_type=F32)


def split2(value):
    high = value.astype(BF16)
    return high, (value - high.astype(F32)).astype(BF16)


def spread_t():
    row = lax.broadcasted_iota(I32, (W, D), 0)
    col = lax.broadcasted_iota(I32, (W, D), 1)
    lane = row & (LANES - 1)
    hit = (lane < USED) & (col == (row >> 7) * USED + lane)
    return jnp.where(hit, 1.0, 0.0).astype(BF16)


def spread():
    row = lax.broadcasted_iota(I32, (D, W), 0)
    col = lax.broadcasted_iota(I32, (D, W), 1)
    lane = col & (LANES - 1)
    hit = (lane < USED) & (row == (col >> 7) * USED + lane)
    return jnp.where(hit, 1.0, 0.0).astype(BF16)


def one_hot(ids_row, rows):
    spot = lax.broadcasted_iota(I32, (rows, ids_row.shape[1]), 0)
    return jnp.where(spot == ids_row, 1.0, 0.0).astype(BF16)


def params():
    return pltpu.CompilerParams(vmem_limit_bytes=VMEM_BYTES)


def full(shape):
    return pl.BlockSpec(shape, lambda i: (0,) * len(shape))


def edge_cols(rows):
    return pl.BlockSpec((rows, BLK), lambda i: (0, i))


def prep_kernel(head_ref, tail_ref, rid_ref, table_ref, counts_ref, uid_ref, slots_ref,
                h_ref, t_ref, r_ref, q_ref, m_ref, pos_ref, target_ref, code_ref,
                pad_ref, high_ref, mid_ref, low_ref):
    put = spread_t()

    @pl.when(pl.program_id(0) == 0)
    def _():
        pad_ref[pl.ds(REL_PAD - 40, 40), :] = jnp.zeros((40, D), F32)
        pad_ref[pl.ds(0, RELS), :] = table_ref[...]
        table = pad_ref[...]
        high = table.astype(BF16)
        rest = table - high.astype(F32)
        mid = rest.astype(BF16)
        low = (rest - mid.astype(F32)).astype(BF16)
        high_ref[...] = dot_nt(put, high).astype(BF16)
        mid_ref[...] = dot_nt(put, mid).astype(BF16)
        low_ref[...] = dot_nt(put, low).astype(BF16)

        counts = jnp.broadcast_to(counts_ref[...], (N_OWN, N_OWN)).astype(F32)
        part = lax.broadcasted_iota(I32, (N_OWN, N_OWN), 0)
        other = lax.broadcasted_iota(I32, (N_OWN, N_OWN), 1)
        ends = jnp.sum(jnp.where(other <= part, counts, 0.0), 1, keepdims=True).astype(I32)
        own = jnp.sum(jnp.where(other == part, counts, 0.0), 1, keepdims=True).astype(I32)
        slots = slots_ref[...]
        target_ref[...] = slots + jnp.sum(jnp.where(slots >= ends, CAP - own, 0), 0, keepdims=True)

        place = lax.broadcasted_iota(I32, (U_CAP, N_OWN), 0)
        lane = (place & (CAP - 1)).astype(F32)
        owner = lax.broadcasted_iota(I32, (U_CAP, N_OWN), 1)
        counts_all = jnp.broadcast_to(counts_ref[...], (U_CAP, N_OWN)).astype(F32)
        start = jnp.sum(jnp.where(owner < (place >> 4), counts_all, 0.0), 1, keepdims=True)
        count = jnp.sum(jnp.where(owner == (place >> 4), counts_all, 0.0), 1, keepdims=True)
        spot = (start + lane[:, :1]).astype(I32)
        column = lax.broadcasted_iota(I32, (U_CAP, U_CAP), 1)
        uid = uid_ref[...].astype(F32)
        picked = jnp.sum(jnp.where(column == spot, uid, 0.0), 1, keepdims=True)
        picked = jnp.where(lane[:, :1] < count, picked, float(ENT_DEV)).astype(I32)
        lanes = lax.broadcasted_iota(I32, (U_CAP, LANES), 1)
        code = jnp.where(lanes == USED, picked >> 5, jnp.where(lanes == USED + 1, picked & 31, 0))
        code_ref[...] = code.astype(F32)

    hit = one_hot(rid_ref[...], REL_PAD)
    rel = dot(high_ref[...], hit) + dot(mid_ref[...], hit) + dot(low_ref[...], hit)
    r_ref[...] = rel
    head = dot_nt(put, head_ref[...])
    tail = dot_nt(put, tail_ref[...])
    h_ref[...] = head.astype(BF16)
    t_ref[...] = tail.astype(BF16)
    hr, hi, tr, ti, rr, ri = head[:HALF], head[HALF:], tail[:HALF], tail[HALF:], rel[:HALF], rel[HALF:]
    qr = (hr * rr - hi * ri).astype(BF16)
    qi = (hr * ri + hi * rr).astype(BF16)
    mr = (rr * tr + ri * ti).astype(BF16)
    mi = (rr * ti - ri * tr).astype(BF16)
    q_ref[pl.ds(0, HALF), :] = qr
    q_ref[pl.ds(HALF, HALF), :] = qi
    m_ref[pl.ds(0, HALF), :] = mr
    m_ref[pl.ds(HALF, HALF), :] = mi
    pos_t = jnp.sum(qr.astype(F32) * tr + qi.astype(F32) * ti, 0, keepdims=True)
    pos_h = jnp.sum(mr.astype(F32) * hr + mi.astype(F32) * hi, 0, keepdims=True)
    side = lax.broadcasted_iota(I32, (8, BLK), 0)
    pos_ref[...] = jnp.where(side == 0, pos_t, pos_h)


def prep(heads, tails, rid, table, counts, uid, slots):
    cols = lambda dt: jax.ShapeDtypeStruct((W, E_DEV), dt)
    return pl.pallas_call(
        prep_kernel,
        name="prep",
        grid=(E_DEV // BLK,),
        in_specs=[
            pl.BlockSpec((BLK, D), lambda i: (i, 0)),
            pl.BlockSpec((BLK, D), lambda i: (i, 0)),
            edge_cols(1),
            full((RELS, D)),
            full((1, N_OWN)),
            full((1, U_CAP)),
            full((1, ROWS + NEG_DEV)),
        ],
        out_specs=[edge_cols(W)] * 5 + [edge_cols(8), full((1, ROWS + NEG_DEV)), full((U_CAP, LANES))],
        out_shape=[
            cols(BF16), cols(BF16), cols(F32), cols(BF16), cols(BF16),
            jax.ShapeDtypeStruct((8, E_DEV), F32),
            jax.ShapeDtypeStruct((1, ROWS + NEG_DEV), I32),
            jax.ShapeDtypeStruct((U_CAP, LANES), F32),
        ],
        scratch_shapes=[pltpu.VMEM((REL_PAD, D), F32)] + [pltpu.VMEM((W, REL_PAD), BF16)] * 3,
        compiler_params=params(),
        cost_estimate=pl.CostEstimate(flops=8 * 10**9, bytes_accessed=8 * 10**6, transcendentals=0),
    )(heads, tails, rid, table, counts, uid, slots)


def score_kernel(n0_ref, n1_ref, n2_ref, n3_ref, q_ref, m_ref, pos_ref,
                 pt_ref, ph_ref, first_ref, own_ref, g1_ref, g2_ref, g3_ref, neg_ref, acc_ref):
    step = pl.program_id(0)

    @pl.when(step == 0)
    def _():
        put = spread()
        for k, ref in enumerate((n0_ref, n1_ref, n2_ref, n3_ref)):
            neg_ref[pl.ds(k * NEG_DEV, NEG_DEV), :] = dot(ref[...], put).astype(BF16)

    neg = neg_ref[...]
    firsts = []
    terms = []
    for side, (query_ref, prob_ref) in enumerate(((q_ref, pt_ref), (m_ref, ph_ref))):
        query = query_ref[...]
        positive = pos_ref[pl.ds(side, 1), :]
        scores = dot(neg, query)
        top = jnp.maximum(positive, jnp.max(scores, 0, keepdims=True))
        weight = jnp.exp(scores - top)
        pos_weight = jnp.exp(positive - top)
        total = pos_weight + jnp.sum(weight, 0, keepdims=True)
        firsts.append(pos_weight / total - 1.0)
        probs = (weight * (1.0 / total)).astype(BF16)
        prob_ref[...] = probs
        terms.append(dot_nt(probs, query))
    row = lax.broadcasted_iota(I32, (8, BLK), 0)
    first_ref[...] = jnp.where(row == 0, firsts[0], firsts[1])
    term = terms[0] + terms[1]

    @pl.when(step == 0)
    def _():
        acc_ref[...] = term

    @pl.when(step > 0)
    def _():
        acc_ref[...] += term

    @pl.when(step == E_DEV // BLK - 1)
    def _():
        own_ref[...] = acc_ref[pl.ds(0, NEG_DEV), :]
        for k, ref in enumerate((g1_ref, g2_ref, g3_ref)):
            ref[...] = acc_ref[pl.ds((k + 1) * NEG_DEV, NEG_DEV), :].astype(BF16)


def score(negs, q, m, pos):
    part = jax.ShapeDtypeStruct((NEG_DEV, W), BF16)
    return pl.pallas_call(
        score_kernel,
        name="score",
        grid=(E_DEV // BLK,),
        in_specs=[full((NEG_DEV, D))] * 4 + [edge_cols(W), edge_cols(W), edge_cols(8)],
        out_specs=[edge_cols(NEG), edge_cols(NEG), edge_cols(8)] + [full((NEG_DEV, W))] * 4,
        out_shape=[
            jax.ShapeDtypeStruct((NEG, E_DEV), BF16),
            jax.ShapeDtypeStruct((NEG, E_DEV), BF16),
            jax.ShapeDtypeStruct((8, E_DEV), F32),
            jax.ShapeDtypeStruct((NEG_DEV, W), F32),
            part, part, part,
        ],
        scratch_shapes=[pltpu.VMEM((NEG, W), BF16), pltpu.VMEM((NEG, W), F32)],
        compiler_params=params(),
        cost_estimate=pl.CostEstimate(flops=5 * 10**9, bytes_accessed=8 * 10**6, transcendentals=2 * 10**6),
    )(*negs, q, m, pos)


def edge_kernel(core_ref, n0_ref, n1_ref, n2_ref, n3_ref, pt_ref, ph_ref, first_ref,
                h_ref, t_ref, r_ref, q_ref, m_ref, rid_ref,
                dhh_ref, dhl_ref, dth_ref, dtl_ref, mine_ref, other_ref, neg_ref):
    step = pl.program_id(0)

    @pl.when(step == 0)
    def _():
        put = spread_t()
        for k, ref in enumerate((n0_ref, n1_ref, n2_ref, n3_ref)):
            neg_ref[:, pl.ds(k * NEG_DEV, NEG_DEV)] = dot_nt(put, ref[...]).astype(BF16)

    neg = neg_ref[...]
    first_t = first_ref[pl.ds(0, 1), :]
    first_h = first_ref[pl.ds(1, 1), :]
    head = h_ref[...].astype(F32)
    tail = t_ref[...].astype(F32)
    rel = r_ref[...]
    query = q_ref[...].astype(F32)
    mirror = m_ref[...].astype(F32)
    dq = first_t * tail + dot(neg, pt_ref[...])
    dm = first_h * head + dot(neg, ph_ref[...])
    hr, hi, tr, ti, rr, ri = head[:HALF], head[HALF:], tail[:HALF], tail[HALF:], rel[:HALF], rel[HALF:]
    qr, qi, mr, mi = dq[:HALF], dq[HALF:], dm[:HALF], dm[HALF:]
    pieces = (
        (dhh_ref, dhl_ref, 0, first_h * mirror[:HALF] + (rr * qr + ri * qi)),
        (dhh_ref, dhl_ref, HALF, first_h * mirror[HALF:] + (rr * qi - ri * qr)),
        (dth_ref, dtl_ref, 0, first_t * query[:HALF] + (rr * mr - ri * mi)),
        (dth_ref, dtl_ref, HALF, first_t * query[HALF:] + (rr * mi + ri * mr)),
    )
    for high_ref, low_ref, at, value in pieces:
        high, low = split2(value)
        high_ref[pl.ds(at, HALF), :] = high
        low_ref[pl.ds(at, HALF), :] = low
    drr = (hr * qr + hi * qi) + (tr * mr + ti * mi)
    dri = (hr * qi - hi * qr) + (ti * mr - tr * mi)
    ids = rid_ref[...] - REL_HALF * core_ref[0]
    ids = jnp.where(ids < 0, ids + REL_PAD, ids)
    hit = one_hot(ids, REL_PAD)
    for at, value in ((0, drr), (HALF, dri)):
        high, low = split2(value)
        term = dot_nt(hit, high) + dot_nt(hit, low)
        for ref, row in ((mine_ref, 0), (other_ref, REL_HALF)):
            @pl.when(step == 0)
            def _(ref=ref, row=row):
                ref[:, pl.ds(at, HALF)] = term[row:row + REL_HALF]

            @pl.when(step > 0)
            def _(ref=ref, row=row):
                ref[:, pl.ds(at, HALF)] += term[row:row + REL_HALF]


def edge(core, negs, pt, ph, first, h, t, r, q, m, rid):
    cols = jax.ShapeDtypeStruct((W, E_DEV), BF16)
    half = jax.ShapeDtypeStruct((REL_HALF, W), F32)
    return pl.pallas_call(
        edge_kernel,
        name="edge",
        grid=(E_DEV // BLK,),
        in_specs=[pl.BlockSpec(memory_space=pltpu.SMEM)] + [full((NEG_DEV, D))] * 4
        + [edge_cols(NEG), edge_cols(NEG), edge_cols(8)] + [edge_cols(W)] * 5 + [edge_cols(1)],
        out_specs=[edge_cols(W)] * 4 + [full((REL_HALF, W))] * 2,
        out_shape=[cols] * 4 + [half] * 2,
        scratch_shapes=[pltpu.VMEM((W, NEG), BF16)],
        compiler_params=params(),
        cost_estimate=pl.CostEstimate(flops=5 * 10**9, bytes_accessed=12 * 10**6, transcendentals=0),
    )(core, *negs, pt, ph, first, h, t, r, q, m, rid)


def slot_kernel(target_h_ref, target_t_ref, dhh_ref, dhl_ref, dth_ref, dtl_ref, out_ref):
    hit_h = one_hot(target_h_ref[...], U_CAP)
    hit_t = one_hot(target_t_ref[...], U_CAP)
    term = (dot_nt(hit_h, dhh_ref[...]) + dot_nt(hit_h, dhl_ref[...])) + (
        dot_nt(hit_t, dth_ref[...]) + dot_nt(hit_t, dtl_ref[...]))

    @pl.when(pl.program_id(0) == 0)
    def _():
        out_ref[...] = term

    @pl.when(pl.program_id(0) > 0)
    def _():
        out_ref[...] += term


def slot(target, dhh, dhl, dth, dtl):
    return pl.pallas_call(
        slot_kernel,
        name="slot",
        grid=(E_DEV // BLK,),
        in_specs=[edge_cols(1), pl.BlockSpec((1, BLK), lambda i: (0, E_DEV // BLK + i))] + [edge_cols(W)] * 4,
        out_specs=full((U_CAP, W)),
        out_shape=jax.ShapeDtypeStruct((U_CAP, W), F32),
        compiler_params=params(),
        cost_estimate=pl.CostEstimate(flops=4 * 10**9, bytes_accessed=5 * 10**6, transcendentals=0),
    )(target, target, dhh, dhl, dth, dtl)


def pack_kernel(target_ref, own_ref, g1_ref, g2_ref, g3_ref, part_ref, code_ref, out_ref):
    rows = own_ref[...] + g1_ref[...].astype(F32) + g2_ref[...].astype(F32) + g3_ref[...].astype(F32)
    high, low = split2(rows)
    hit = one_hot(target_ref[...], U_CAP)
    total = part_ref[...] + (dot(hit, high) + dot(hit, low))
    code = code_ref[...]
    for k in range(N_GRP):
        out_ref[k] = (total[:, k * LANES:(k + 1) * LANES] + code).astype(BF16)


def pack(target, own, g1, g2, g3, part, code):
    return pl.pallas_call(
        pack_kernel,
        name="pack",
        grid=(1,),
        in_specs=[pl.BlockSpec((1, NEG_DEV), lambda i: (0, ROWS // NEG_DEV))] + [full((NEG_DEV, W))] * 4
        + [full((U_CAP, W)), full((U_CAP, LANES))],
        out_specs=full((N_GRP, U_CAP, LANES)),
        out_shape=jax.ShapeDtypeStruct((N_GRP, U_CAP, LANES), BF16),
        compiler_params=params(),
        cost_estimate=pl.CostEstimate(flops=10**9, bytes_accessed=5 * 10**6, transcendentals=0),
    )(target, own, g1, g2, g3, part, code)


def partition_kernel(rows_ref, out_ref, acc_ref):
    step = pl.program_id(0)
    rows = rows_ref[...]
    lane = lax.broadcasted_iota(I32, (8, LANES), 1)
    weight = jnp.where(lane == USED, 32.0, jnp.where(lane == USED + 1, 1.0, 0.0)).astype(BF16)
    ids = dot_nt(weight, rows)[:1].astype(I32)
    term = dot(one_hot(ids, ENT_DEV), rows)

    @pl.when(step == 0)
    def _():
        acc_ref[...] = term

    @pl.when(step > 0)
    def _():
        acc_ref[...] += term

    @pl.when(step == pl.num_programs(0) - 1)
    def _():
        out_ref[...] = acc_ref[:, :USED]


def partition(rows):
    block = 1024
    return pl.pallas_call(
        partition_kernel,
        name="partition",
        grid=(rows.shape[0] // block,),
        in_specs=[pl.BlockSpec((block, LANES), lambda i: (i, 0))],
        out_specs=full((ENT_DEV, USED)),
        out_shape=jax.ShapeDtypeStruct((ENT_DEV, USED), F32),
        scratch_shapes=[pltpu.VMEM((ENT_DEV, LANES), F32)],
        compiler_params=params(),
        cost_estimate=pl.CostEstimate(flops=2 * 10**9, bytes_accessed=2 * 10**6, transcendentals=0),
    )(rows)


def rel_x_kernel(grp_ref, mine_ref, other_ref, own_ref, o1_ref, o2_ref, o3_ref):
    for k, ref in enumerate((own_ref, o1_ref, o2_ref, o3_ref)):
        at = pl.multiple_of(((grp_ref[0] + k) & (N_GRP - 1)) * LANES, LANES)
        total = mine_ref[:, pl.ds(at, LANES)] + other_ref[:, pl.ds(at, LANES)]
        ref[...] = total.astype(ref.dtype)


def rel_x(grp, mine, other):
    part = jax.ShapeDtypeStruct((REL_HALF, LANES), BF16)
    return pl.pallas_call(
        rel_x_kernel,
        name="rel_x",
        grid=(1,),
        in_specs=[pl.BlockSpec(memory_space=pltpu.SMEM)] + [full((REL_HALF, W))] * 2,
        out_specs=[full((REL_HALF, LANES))] * 4,
        out_shape=[jax.ShapeDtypeStruct((REL_HALF, LANES), F32), part, part, part],
        compiler_params=params(),
        cost_estimate=pl.CostEstimate(flops=10**6, bytes_accessed=4 * 10**6, transcendentals=0),
    )(grp, mine, other)


def rel_yz_kernel(own_ref, i1_ref, i2_ref, i3_ref, out_ref):
    out_ref[...] = own_ref[...] + i1_ref[...].astype(F32) + i2_ref[...].astype(F32) + i3_ref[...].astype(F32)


def rel_yz(own, i1, i2, i3):
    return pl.pallas_call(
        rel_yz_kernel,
        name="rel_yz",
        grid=(1,),
        in_specs=[full((REL_HALF, LANES))] * 4,
        out_specs=full((REL_HALF, LANES)),
        out_shape=jax.ShapeDtypeStruct((REL_HALF, LANES), F32),
        compiler_params=params(),
        cost_estimate=pl.CostEstimate(flops=10**6, bytes_accessed=2 * 10**6, transcendentals=0),
    )(own, i1, i2, i3)


def rel_sum_kernel(in_ref, out_ref):
    total = jnp.sum(in_ref[...], 0).astype(BF16)
    out_ref[...] = jnp.broadcast_to(total[None], out_ref.shape)


def rel_sum(parts):
    return pl.pallas_call(
        rel_sum_kernel,
        name="rel_sum",
        grid=(1,),
        in_specs=[full(parts.shape)],
        out_specs=full(parts.shape),
        out_shape=jax.ShapeDtypeStruct(parts.shape, BF16),
        compiler_params=params(),
        cost_estimate=pl.CostEstimate(flops=10**6, bytes_accessed=10**6, transcendentals=0),
    )(parts)


def table_kernel(place_ref, *refs):
    out_ref = refs[-1]
    core = place_ref[0]
    grp = place_ref[1]
    row = lax.broadcasted_iota(I32, (LANES, D), 0)
    col = lax.broadcasted_iota(I32, (LANES, D), 1)
    for half in range(2):
        total = jnp.zeros((REL_HALF, D), F32)
        for k in range(N_GRP):
            at = ((grp - k) & (N_GRP - 1)) * USED
            put = jnp.where((row < USED) & (col == row + at), 1.0, 0.0).astype(BF16)
            total = total + dot(refs[half * N_GRP + k][...], put)

        @pl.when(core == half)
        def _():
            out_ref[pl.ds(0, REL_HALF), :] = total

        @pl.when(core != half)
        def _():
            out_ref[pl.ds(REL_HALF, RELS - REL_HALF), :] = total[:RELS - REL_HALF]


def table(place, blocks):
    return pl.pallas_call(
        table_kernel,
        name="table",
        grid=(1,),
        in_specs=[pl.BlockSpec(memory_space=pltpu.SMEM)] + [full((REL_HALF, LANES))] * 8,
        out_specs=full((RELS, D)),
        out_shape=jax.ShapeDtypeStruct((RELS, D), F32),
        compiler_params=params(),
        cost_estimate=pl.CostEstimate(flops=10**9, bytes_accessed=4 * 10**6, transcendentals=0),
    )(place, *blocks)


def ring(value, k):
    return lax.ppermute(value, "x", [(i, (i + k) % N_GRP) for i in range(N_GRP)])


def pair(value):
    return lax.ppermute(value, "c", [(0, 1), (1, 0)])


def shards(head_rows, tail_rows, rel_ids, neg_rows, rel_table, owner_counts, unique_ids, head_slot, tail_slot, negative_slot):
    core = lax.axis_index("c").astype(I32)
    grp = lax.axis_index("x").astype(I32)
    negs = [neg_rows] + [ring(neg_rows, k) for k in (1, 2, 3)]
    rid = rel_ids.reshape(1, -1)
    slots = jnp.concatenate([head_slot, tail_slot, negative_slot]).reshape(1, -1)
    h, t, r, q, m, pos, target, code = prep(head_rows, tail_rows, rid, rel_table, owner_counts, unique_ids, slots)
    pt, ph, first, own, g1, g2, g3 = score(negs, q, m, pos)
    back = [ring(g, N_GRP - k) for k, g in ((1, g1), (2, g2), (3, g3))]
    dhh, dhl, dth, dtl, mine, other = edge(core.reshape(1), negs, pt, ph, first, h, t, r, q, m, rid)
    other = pair(other)
    part = slot(target, dhh, dhl, dth, dtl)
    rel_own, o1, o2, o3 = rel_x(grp.reshape(1), mine, other)
    arrived = [ring(o, k) for k, o in ((1, o1), (2, o2), (3, o3))]
    packed = pack(target, own, *back, part, code)
    received = lax.all_to_all(packed.reshape(N_GRP * N_OWN, CAP, LANES), ALL, 0, 0, tiled=True)
    chip = rel_yz(rel_own, *arrived).reshape(N_YZ, REL_HALF // N_YZ, LANES)
    chip = rel_sum(lax.all_to_all(chip, ("y", "z"), 0, 0, tiled=True))
    chip = lax.all_to_all(chip, ("y", "z"), 0, 0, tiled=True).reshape(REL_HALF, LANES)
    quarter = [chip] + [ring(chip, k) for k in (1, 2, 3)]
    blocks = quarter + [pair(value) for value in quarter]
    rel_grad = table(jnp.stack([core, grp]), blocks)
    entity_grad = partition(received.reshape(-1, LANES))
    return entity_grad, rel_grad


def solution(mesh):
    split = Mesh(mesh.devices.reshape(N_GRP, 4, 8, 2), ALL)
    edges = P(ALL)
    rows = P(ALL, None)
    in_specs = (rows, rows, edges, rows, P(), rows, rows, edges, edges, edges)
    out_specs = (P(("y", "z", "c"), "x"), P())
    return jax.shard_map(shards, mesh=split, in_specs=in_specs, out_specs=out_specs, check_vma=False)
```

```python
import jax
import jax.numpy as jnp
from jax import lax
from jax.experimental import pallas as pl
from jax.experimental.pallas import tpu as pltpu
from jax.sharding import Mesh
from jax.sharding import PartitionSpec as P

D = 400
HALF = D // 2
RELS = 1500
E_DEV = 768
ENT_DEV = 1024
NEG_DEV = 256
CAP = 16
NEG = 1024
U_CAP = 1024
N_GRP = 4
N_OWN = 64
N_XY = 16
LANES = 128
USED = D // N_GRP
REL_PAD = 1536
REL_HALF = REL_PAD // 2
REL_TILES = REL_HALF // 128
REL_PART = 160
ROWS = 2 * E_DEV
ALL = ("x", "y", "z", "c")
F32 = jnp.float32
BF16 = jnp.bfloat16
I32 = jnp.int32


def dot(a, b):
    return lax.dot_general(a, b, (((1,), (0,)), ((), ())), preferred_element_type=F32)


def dot_nt(a, b):
    return lax.dot_general(a, b, (((1,), (1,)), ((), ())), preferred_element_type=F32)


def split2(value):
    high = value.astype(BF16)
    return high, (value - high.astype(F32)).astype(BF16)


def eye(size):
    row = lax.broadcasted_iota(I32, (size, size), 0)
    col = lax.broadcasted_iota(I32, (size, size), 1)
    return jnp.where(row == col, 1.0, 0.0).astype(BF16)


def one_hot(ids_row, rows):
    spot = lax.broadcasted_iota(I32, (LANES, ids_row.shape[1]), 0).astype(BF16)
    blocks = []
    for at in range(0, rows, LANES):
        here = jnp.clip(ids_row - at, -1, LANES).astype(BF16)
        blocks.append(jnp.where(spot == here, jnp.ones((), BF16), jnp.zeros((), BF16)))
    return jnp.concatenate(blocks, 0)


def full(shape):
    return pl.BlockSpec(shape, lambda i: (0,) * len(shape))


def arr(shape, dtype):
    return jax.ShapeDtypeStruct(shape, dtype)


def call(kernel, name, grid, in_specs, out_specs, out_shape, scratch=(), mib=60, flops=10**6):
    return pl.pallas_call(
        kernel,
        name=name,
        grid=(grid,),
        in_specs=in_specs,
        out_specs=out_specs,
        out_shape=out_shape,
        scratch_shapes=list(scratch),
        compiler_params=pltpu.CompilerParams(vmem_limit_bytes=mib * 1024 * 1024),
        cost_estimate=pl.CostEstimate(flops=flops, bytes_accessed=10**5, transcendentals=0),
    )


SMEM = pl.BlockSpec(memory_space=pltpu.SMEM)


def prep_kernel(head_ref, tail_ref, rid_ref, table_ref, counts_ref, uid_ref, hs_ref, ts_ref, ns_ref,
                r_ref, q_ref, m_ref, pos_ref, rids_ref, th_ref, tt_ref, tn_ref, code_ref,
                high_ref, mid_ref, low_ref):
    table = table_ref[...]
    high = table.astype(BF16)
    rest = table - high.astype(F32)
    mid = rest.astype(BF16)
    low = (rest - mid.astype(F32)).astype(BF16)
    for ref, value in ((high_ref, high), (mid_ref, mid), (low_ref, low)):
        ref[:, pl.ds(REL_PAD - LANES, LANES)] = jnp.zeros((D, LANES), BF16)
        ref[:, pl.ds(0, RELS)] = value

    rids_ref[...] = rid_ref[...].reshape(1, E_DEV)
    counts = jnp.broadcast_to(counts_ref[...], (N_OWN, N_OWN)).astype(F32)
    part = lax.broadcasted_iota(I32, (N_OWN, N_OWN), 0)
    other = lax.broadcasted_iota(I32, (N_OWN, N_OWN), 1)
    ends = jnp.sum(jnp.where(other <= part, counts, 0.0), 1, keepdims=True).astype(I32)
    own = jnp.sum(jnp.where(other == part, counts, 0.0), 1, keepdims=True).astype(I32)
    for out, ref in ((th_ref, hs_ref), (tt_ref, ts_ref), (tn_ref, ns_ref)):
        slots = ref[...].reshape(1, -1)
        out[...] = slots + jnp.sum(jnp.where(slots >= ends, CAP - own, 0), 0, keepdims=True)

    place = lax.broadcasted_iota(I32, (U_CAP, N_OWN), 0)
    lane = (place & (CAP - 1)).astype(F32)
    owner = lax.broadcasted_iota(I32, (U_CAP, N_OWN), 1)
    counts_all = jnp.broadcast_to(counts_ref[...], (U_CAP, N_OWN)).astype(F32)
    start = jnp.sum(jnp.where(owner < (place >> 4), counts_all, 0.0), 1, keepdims=True)
    count = jnp.sum(jnp.where(owner == (place >> 4), counts_all, 0.0), 1, keepdims=True)
    spot = (start + lane[:, :1]).astype(I32)
    column = lax.broadcasted_iota(I32, (U_CAP, U_CAP), 1)
    uid = uid_ref[...].astype(F32)
    picked = jnp.sum(jnp.where(column == spot, uid, 0.0), 1, keepdims=True)
    picked = jnp.where(lane[:, :1] < count, picked, float(ENT_DEV)).astype(I32)
    lanes = lax.broadcasted_iota(I32, (U_CAP, LANES), 1)
    code = jnp.where(lanes == USED, picked >> 5, jnp.where(lanes == USED + 1, picked & 31, 0))
    code_ref[...] = code.astype(F32)

    hit = one_hot(rids_ref[...], REL_PAD)
    rel = dot(high_ref[...], hit) + dot(mid_ref[...], hit) + dot(low_ref[...], hit)
    r_ref[...] = rel
    head = head_ref[...].astype(F32)
    tail = tail_ref[...].astype(F32)
    hr, hi, tr, ti, rr, ri = head[:HALF], head[HALF:], tail[:HALF], tail[HALF:], rel[:HALF], rel[HALF:]
    query = jnp.concatenate([hr * rr - hi * ri, hr * ri + hi * rr], 0).astype(BF16)
    mirror = jnp.concatenate([rr * tr + ri * ti, rr * ti - ri * tr], 0).astype(BF16)
    q_ref[...] = query
    m_ref[...] = mirror
    pos_t = jnp.sum(query.astype(F32) * tail, 0, keepdims=True)
    pos_h = jnp.sum(mirror.astype(F32) * head, 0, keepdims=True)
    side = lax.broadcasted_iota(I32, (8, E_DEV), 0)
    pos_ref[...] = jnp.where(side == 0, pos_t, pos_h)


def prep(heads, tails, rid, table, counts, uid, hs, ts, ns):
    cols = lambda dt: arr((D, E_DEV), dt)
    return call(
        prep_kernel, "prep", 1,
        [full((D, E_DEV)), full((D, E_DEV)), full((E_DEV,)), full((D, RELS)), full((1, N_OWN)), full((1, U_CAP)),
         full((E_DEV,)), full((E_DEV,)), full((NEG_DEV,))],
        [full((D, E_DEV))] * 3 + [full((8, E_DEV))] + [full((1, E_DEV))] * 3 + [full((1, NEG_DEV)), full((U_CAP, LANES))],
        [cols(F32), cols(BF16), cols(BF16), arr((8, E_DEV), F32),
         arr((1, E_DEV), I32), arr((1, E_DEV), I32), arr((1, E_DEV), I32), arr((1, NEG_DEV), I32), arr((U_CAP, LANES), F32)],
        [pltpu.VMEM((D, REL_PAD), BF16)] * 3,
    )(heads, tails, rid, table, counts, uid, hs, ts, ns)


def edge_kernel(core_ref, n0_ref, n1_ref, n2_ref, n3_ref, head_ref, tail_ref, r_ref, q_ref, m_ref, pos_ref, rid_ref,
                pt_ref, ph_ref, first_ref, dq_ref, dm_ref, mine_ref, other_ref, neg_ref, turned_ref):
    turn = eye(NEG_DEV)
    for k, ref in enumerate((n0_ref, n1_ref, n2_ref, n3_ref)):
        value = ref[...]
        neg_ref[:, pl.ds(k * NEG_DEV, NEG_DEV)] = value
        turned_ref[pl.ds(k * NEG_DEV, NEG_DEV), :] = dot_nt(turn, value).astype(BF16)

    head = head_ref[...].astype(F32)
    tail = tail_ref[...].astype(F32)
    firsts = []
    for side, (query_ref, positives, prob_ref, grad_ref) in enumerate((
            (q_ref, tail, pt_ref, dq_ref), (m_ref, head, ph_ref, dm_ref))):
        positive = pos_ref[pl.ds(side, 1), :]
        scores = dot(turned_ref[...], query_ref[...])
        top = jnp.maximum(positive, jnp.max(scores, 0, keepdims=True))
        weight = jnp.exp(scores - top)
        pos_weight = jnp.exp(positive - top)
        total = pos_weight + jnp.sum(weight, 0, keepdims=True)
        first = pos_weight / total - 1.0
        probs = (weight * (1.0 / total)).astype(BF16)
        prob_ref[...] = probs
        grad_ref[...] = first * positives + dot(neg_ref[...], probs)
        firsts.append(first)
    row = lax.broadcasted_iota(I32, (8, E_DEV), 0)
    first_ref[...] = jnp.where(row == 0, firsts[0], firsts[1])

    hr, hi, tr, ti = head[:HALF], head[HALF:], tail[:HALF], tail[HALF:]
    qr, qi, mr, mi = dq_ref[:HALF], dq_ref[HALF:], dm_ref[:HALF], dm_ref[HALF:]
    d_rel = jnp.concatenate([(hr * qr + hi * qi) + (tr * mr + ti * mi), (hr * qi - hi * qr) + (ti * mr - tr * mi)], 0)
    ids = rid_ref[...] - REL_HALF * core_ref[0]
    ids = jnp.where(ids < 0, ids + REL_PAD, ids)
    hit = one_hot(ids, REL_PAD)
    high, low = split2(d_rel)
    for ref, at in ((other_ref, REL_HALF), (mine_ref, 0)):
        part = hit[at:at + REL_HALF]
        ref[...] = (dot_nt(part, high) + dot_nt(part, low)).T


def edge(core, negs, h, t, r, q, m, pos, rid):
    part = (D, NEG_DEV)
    cols = (D, E_DEV)
    half = (D, REL_HALF)
    return call(
        edge_kernel, "edge", 1,
        [SMEM] + [full(part)] * 4 + [full(cols)] * 5 + [full((8, E_DEV)), full((1, E_DEV))],
        [full((NEG, E_DEV))] * 2 + [full((8, E_DEV))] + [full(cols)] * 2 + [full(half)] * 2,
        [arr((NEG, E_DEV), BF16)] * 2 + [arr((8, E_DEV), F32)] + [arr(cols, F32)] * 2 + [arr(half, F32)] * 2,
        [pltpu.VMEM((D, NEG), BF16), pltpu.VMEM((NEG, D), BF16)],
        flops=10**10,
    )(core, *negs, h, t, r, q, m, pos, rid)


def group_kernel(q_ref, m_ref, pt_ref, ph_ref, own_ref, g1_ref, g2_ref, g3_ref):
    term = dot_nt(q_ref[...], pt_ref[...]) + dot_nt(m_ref[...], ph_ref[...])
    own_ref[...] = term[:, :NEG_DEV]
    for k, ref in enumerate((g1_ref, g2_ref, g3_ref)):
        ref[...] = term[:, (k + 1) * NEG_DEV:(k + 2) * NEG_DEV].astype(BF16)


def group(q, m, pt, ph):
    part = (D, NEG_DEV)
    return call(
        group_kernel, "group", 1,
        [full((D, E_DEV))] * 2 + [full((NEG, E_DEV))] * 2, [full(part)] * 4, [arr(part, F32)] + [arr(part, BF16)] * 3,
        flops=4 * 10**9,
    )(q, m, pt, ph)


def slot_kernel(target_h_ref, target_t_ref, first_ref, dq_ref, dm_ref, r_ref, q_ref, m_ref, code_ref, out_ref):
    rel = r_ref[...]
    dq = dq_ref[...]
    dm = dm_ref[...]
    rr, ri, qr, qi, mr, mi = rel[:HALF], rel[HALF:], dq[:HALF], dq[HALF:], dm[:HALF], dm[HALF:]
    d_head = first_ref[pl.ds(1, 1), :] * m_ref[...].astype(F32) + jnp.concatenate([rr * qr + ri * qi, rr * qi - ri * qr], 0)
    d_tail = first_ref[pl.ds(0, 1), :] * q_ref[...].astype(F32) + jnp.concatenate([rr * mr - ri * mi, rr * mi + ri * mr], 0)
    hit_h = one_hot(target_h_ref[...], U_CAP)
    hit_t = one_hot(target_t_ref[...], U_CAP)
    head_high, head_low = split2(d_head)
    tail_high, tail_low = split2(d_tail)
    total = (dot_nt(hit_h, head_high) + dot_nt(hit_h, head_low)) + (dot_nt(hit_t, tail_high) + dot_nt(hit_t, tail_low))
    code = code_ref[:, USED:]
    for k in range(N_GRP):
        out_ref[k] = jnp.concatenate([total[:, k * USED:(k + 1) * USED], code], 1)


def slot(th, tt, first, dq, dm, r, q, m, code):
    cols = full((D, E_DEV))
    shape = (N_GRP, U_CAP, LANES)
    return call(
        slot_kernel, "slot", 1,
        [full((1, E_DEV))] * 2 + [full((8, E_DEV))] + [cols] * 5 + [full((U_CAP, LANES))],
        full(shape), arr(shape, F32),
        flops=8 * 10**9,
    )(th, tt, first, dq, dm, r, q, m, code)


def pack_kernel(target_ref, own_ref, g1_ref, g2_ref, g3_ref, part_ref, out_ref):
    rows = own_ref[...] + g1_ref[...].astype(F32) + g2_ref[...].astype(F32) + g3_ref[...].astype(F32)
    hit = one_hot(target_ref[...], U_CAP)
    rest = jnp.zeros((LANES - USED, NEG_DEV), F32)
    for k in range(N_GRP):
        high, low = split2(jnp.concatenate([rows[k * USED:(k + 1) * USED], rest], 0))
        out_ref[k] = (part_ref[k] + (dot_nt(hit, high) + dot_nt(hit, low))).astype(BF16)


def pack(tn, own, g1, g2, g3, part):
    shape = (N_GRP, U_CAP, LANES)
    return call(
        pack_kernel, "pack", 1,
        [full((1, NEG_DEV))] + [full((D, NEG_DEV))] * 4 + [full(shape)],
        full(shape), arr(shape, BF16),
        flops=3 * 10**9,
    )(tn, own, g1, g2, g3, part)


def partition_kernel(rows_ref, out_ref, acc_ref):
    step = pl.program_id(0)
    rows = rows_ref[...]
    lane = lax.broadcasted_iota(I32, (8, LANES), 1)
    weight = jnp.where(lane == USED, 32.0, jnp.where(lane == USED + 1, 1.0, 0.0)).astype(BF16)
    ids = dot_nt(weight, rows)[:1].astype(I32)
    term = dot(one_hot(ids, ENT_DEV), rows)

    @pl.when(step == 0)
    def _():
        acc_ref[...] = term

    @pl.when(step > 0)
    def _():
        acc_ref[...] += term

    @pl.when(step == pl.num_programs(0) - 1)
    def _():
        out_ref[...] = acc_ref[...].T[:USED]


def partition(rows):
    block = 1024
    return call(
        partition_kernel, "partition", rows.shape[0] // block,
        [pl.BlockSpec((block, LANES), lambda i: (i, 0))],
        full((USED, ENT_DEV)),
        arr((USED, ENT_DEV), F32),
        [pltpu.VMEM((ENT_DEV, LANES), F32)],
    )(rows)


def rel_chip_kernel(mine_ref, other_ref, out_ref):
    for k in range(REL_TILES):
        at = pl.ds(k * LANES, LANES)
        out_ref[pl.ds(k * D, D), :] = (mine_ref[:, at] + other_ref[:, at]).astype(BF16)
    rest = N_XY * REL_PART - REL_TILES * D
    out_ref[pl.ds(REL_TILES * D, rest), :] = jnp.zeros((rest, LANES), BF16)


def rel_chip(mine, other):
    shape = (N_XY * REL_PART, LANES)
    return call(rel_chip_kernel, "rel_chip", 1, [full((D, REL_HALF))] * 2, full(shape), arr(shape, BF16), mib=24)(mine, other)


def rel_xy_kernel(in_ref, out_ref):
    total = jnp.sum(in_ref[...].astype(F32), 0).astype(BF16)
    out_ref[...] = jnp.broadcast_to(total[None], out_ref.shape)


def rel_xy(parts):
    shape = (REL_PART, LANES)
    return call(rel_xy_kernel, "rel_xy", 1, [full((N_XY,) + shape)], full((8,) + shape), arr((8,) + shape, BF16), mib=24)(parts)


def rel_z_kernel(in_ref, out_ref):
    out_ref[...] = jnp.sum(in_ref[...].astype(F32), 0).astype(BF16)


def rel_z(parts):
    shape = (REL_PART, LANES)
    return call(rel_z_kernel, "rel_z", 1, [full((8,) + shape)], full(shape), arr(shape, BF16), mib=24)(parts)


def place_kernel(me_ref, *refs):
    out_ref = refs[-1]
    rows = refs[0].shape[0]
    for k, ref in enumerate(refs[:-1]):
        at = pl.multiple_of(((me_ref[0] - k) & (N_GRP - 1)) * rows, rows)
        out_ref[pl.ds(at, rows), :] = ref[...]


def place(me, blocks, name):
    rows = blocks[0].shape[0]
    shape = (rows * N_GRP, LANES)
    return call(
        place_kernel, name, 1, [SMEM] + [full((rows, LANES))] * N_GRP, full(shape), arr(shape, BF16), mib=24
    )(me, *blocks)


def table_kernel(core_ref, mine_ref, other_ref, out_ref):
    for half, ref in enumerate((mine_ref, other_ref)):
        for place in range(2):
            @pl.when((core_ref[0] == half) == (place == 0))
            def _(ref=ref, place=place):
                for k in range(REL_TILES):
                    at = place * REL_HALF + k * LANES
                    width = min(LANES, RELS - at)
                    out_ref[:, pl.ds(at, width)] = ref[pl.ds(k * D, D), :].astype(F32)[:, :width]


def table(core, mine, other):
    return call(
        table_kernel, "table", 1, [SMEM] + [full((N_XY * REL_PART, LANES))] * 2, full((D, RELS)), arr((D, RELS), F32)
    )(core, mine, other)


def shift(value, axis, k):
    return lax.ppermute(value, axis, [(i, (i + k) % N_GRP) for i in range(N_GRP)])


def pair(value):
    return lax.ppermute(value, "c", [(0, 1), (1, 0)])


def around(value, axis):
    return [value] + [shift(value, axis, k) for k in (1, 2, 3)]


def shards(head_rows, tail_rows, rel_ids, neg_rows, rel_table, owner_counts, unique_ids, head_slot, tail_slot, negative_slot):
    core = lax.axis_index("c").astype(I32).reshape(1)
    x = lax.axis_index("x").astype(I32).reshape(1)
    y = lax.axis_index("y").astype(I32).reshape(1)
    heads, tails = head_rows.T, tail_rows.T
    negs = around(neg_rows.T, "x")
    r, q, m, pos, rid, th, tt, tn, code = prep(
        heads, tails, rel_ids, rel_table.T, owner_counts, unique_ids, head_slot, tail_slot, negative_slot)
    pt, ph, first, dq, dm, mine, other = edge(core, negs, heads, tails, r, q, m, pos, rid)
    own, g1, g2, g3 = group(q, m, pt, ph)
    back = [shift(g, "x", N_GRP - k) for k, g in ((1, g1), (2, g2), (3, g3))]
    other = pair(other)
    mine, other, own = lax.optimization_barrier((mine, other, own))
    chip = rel_chip(mine, other).reshape(N_XY, REL_PART, LANES)
    part = slot(th, tt, first, dq, dm, r, q, m, code)
    chip = lax.all_to_all(chip, ("x", "y"), 0, 0, tiled=True)
    chip, part, *back = lax.optimization_barrier((chip, part, *back))
    column = lax.all_to_all(rel_xy(chip), "z", 0, 0, tiled=True)
    piece = rel_z(column)
    packed = pack(tn, own, *back, part)
    piece, packed = lax.optimization_barrier((piece, packed))
    received = lax.all_to_all(packed.reshape(N_GRP * N_OWN, CAP, LANES), ALL, 0, 0, tiled=True)
    quarter = place(y, around(piece, "y"), "place_y")
    half = place(x, around(quarter, "x"), "place_x")
    rel_grad = table(core, half, pair(half))
    entity_grad = partition(received.reshape(-1, LANES))
    return entity_grad.T, rel_grad.T


def solution(mesh):
    split = Mesh(mesh.devices.reshape(N_GRP, 4, 8, 2), ALL)
    edges = P(ALL)
    rows = P(ALL, None)
    in_specs = (rows, rows, edges, rows, P(), rows, rows, edges, edges, edges)
    out_specs = (P(("y", "z", "c"), "x"), P())
    return jax.shard_map(shards, mesh=split, in_specs=in_specs, out_specs=out_specs, check_vma=False)
```

```python
import jax
import jax.numpy as jnp
from jax import lax
from jax.experimental import pallas as pl
from jax.experimental.pallas import tpu as pltpu
from jax.sharding import Mesh
from jax.sharding import PartitionSpec as P

D = 400
HALF = D // 2
RELS = 1500
E_DEV = 768
ENT_DEV = 1024
NEG_DEV = 256
CAP = 16
NEG = 1024
U_CAP = 1024
N_GRP = 4
N_OWN = 64
N_XY = 16
LANES = 128
USED = D // N_GRP
REL_PAD = 1536
REL_HALF = REL_PAD // 2
REL_TILES = REL_HALF // 128
REL_PART = 160
AT_UID = 3 * E_DEV + NEG_DEV
AT_COUNTS = AT_UID + U_CAP
INTS = AT_COUNTS + 128
ALL = ("x", "y", "z", "c")
F32 = jnp.float32
BF16 = jnp.bfloat16
I32 = jnp.int32


def dot(a, b):
    return lax.dot_general(a, b, (((1,), (0,)), ((), ())), preferred_element_type=F32)


def dot_nt(a, b):
    return lax.dot_general(a, b, (((1,), (1,)), ((), ())), preferred_element_type=F32)


def split2(value):
    high = value.astype(BF16)
    return high, (value - high.astype(F32)).astype(BF16)


def eye(size):
    row = lax.broadcasted_iota(I32, (size, size), 0)
    col = lax.broadcasted_iota(I32, (size, size), 1)
    return jnp.where(row == col, 1.0, 0.0).astype(BF16)


def one_hot(ids_row, rows):
    spot = lax.broadcasted_iota(I32, (LANES, ids_row.shape[1]), 0).astype(BF16)
    blocks = []
    for at in range(0, rows, LANES):
        here = jnp.clip(ids_row - at, -1, LANES).astype(BF16)
        blocks.append(jnp.where(spot == here, jnp.ones((), BF16), jnp.zeros((), BF16)))
    return jnp.concatenate(blocks, 0)


def full(shape):
    return pl.BlockSpec(shape, lambda i: (0,) * len(shape))


def arr(shape, dtype):
    return jax.ShapeDtypeStruct(shape, dtype)


def call(kernel, name, grid, in_specs, out_specs, out_shape, scratch=(), mib=60, flops=10**6):
    return pl.pallas_call(
        kernel,
        name=name,
        grid=(grid,),
        in_specs=in_specs,
        out_specs=out_specs,
        out_shape=out_shape,
        scratch_shapes=list(scratch),
        compiler_params=pltpu.CompilerParams(vmem_limit_bytes=mib * 1024 * 1024),
        cost_estimate=pl.CostEstimate(flops=flops, bytes_accessed=10**5, transcendentals=0),
    )


SMEM = pl.BlockSpec(memory_space=pltpu.SMEM)


def prep_kernel(head_ref, tail_ref, table_ref, ints_ref,
                r_ref, q_ref, m_ref, pos_ref, rids_ref, th_ref, tt_ref, tn_ref, code_ref,
                high_ref, mid_ref, low_ref):
    table = table_ref[...]
    high = table.astype(BF16)
    rest = table - high.astype(F32)
    mid = rest.astype(BF16)
    low = (rest - mid.astype(F32)).astype(BF16)
    for ref, value in ((high_ref, high), (mid_ref, mid), (low_ref, low)):
        ref[:, pl.ds(REL_PAD - LANES, LANES)] = jnp.zeros((D, LANES), BF16)
        ref[:, pl.ds(0, RELS)] = value

    rids_ref[...] = ints_ref[:, :E_DEV]
    counts_row = ints_ref[:, AT_COUNTS:AT_COUNTS + N_OWN]
    counts = jnp.broadcast_to(counts_row, (N_OWN, N_OWN)).astype(F32)
    part = lax.broadcasted_iota(I32, (N_OWN, N_OWN), 0)
    other = lax.broadcasted_iota(I32, (N_OWN, N_OWN), 1)
    ends = jnp.sum(jnp.where(other <= part, counts, 0.0), 1, keepdims=True).astype(I32)
    own = jnp.sum(jnp.where(other == part, counts, 0.0), 1, keepdims=True).astype(I32)
    for out, at in ((th_ref, E_DEV), (tt_ref, 2 * E_DEV), (tn_ref, 3 * E_DEV)):
        slots = ints_ref[:, at:at + out.shape[1]]
        out[...] = slots + jnp.sum(jnp.where(slots >= ends, CAP - own, 0), 0, keepdims=True)

    place = lax.broadcasted_iota(I32, (U_CAP, N_OWN), 0)
    lane = (place & (CAP - 1)).astype(F32)
    owner = lax.broadcasted_iota(I32, (U_CAP, N_OWN), 1)
    counts_all = jnp.broadcast_to(counts_row, (U_CAP, N_OWN)).astype(F32)
    start = jnp.sum(jnp.where(owner < (place >> 4), counts_all, 0.0), 1, keepdims=True)
    count = jnp.sum(jnp.where(owner == (place >> 4), counts_all, 0.0), 1, keepdims=True)
    spot = (start + lane[:, :1]).astype(I32)
    column = lax.broadcasted_iota(I32, (U_CAP, U_CAP), 1)
    uid = ints_ref[:, AT_UID:AT_UID + U_CAP].astype(F32)
    picked = jnp.sum(jnp.where(column == spot, uid, 0.0), 1, keepdims=True)
    picked = jnp.where(lane[:, :1] < count, picked, float(ENT_DEV)).astype(I32)
    lanes = lax.broadcasted_iota(I32, (U_CAP, LANES), 1)
    code = jnp.where(lanes == USED, picked >> 5, jnp.where(lanes == USED + 1, picked & 31, 0))
    code_ref[...] = code.astype(F32)

    hit = one_hot(rids_ref[...], REL_PAD)
    rel = dot(high_ref[...], hit) + dot(mid_ref[...], hit) + dot(low_ref[...], hit)
    r_ref[...] = rel
    head = head_ref[...].astype(F32)
    tail = tail_ref[...].astype(F32)
    hr, hi, tr, ti, rr, ri = head[:HALF], head[HALF:], tail[:HALF], tail[HALF:], rel[:HALF], rel[HALF:]
    query = jnp.concatenate([hr * rr - hi * ri, hr * ri + hi * rr], 0).astype(BF16)
    mirror = jnp.concatenate([rr * tr + ri * ti, rr * ti - ri * tr], 0).astype(BF16)
    q_ref[...] = query
    m_ref[...] = mirror
    pos_t = jnp.sum(query.astype(F32) * tail, 0, keepdims=True)
    pos_h = jnp.sum(mirror.astype(F32) * head, 0, keepdims=True)
    side = lax.broadcasted_iota(I32, (8, E_DEV), 0)
    pos_ref[...] = jnp.where(side == 0, pos_t, pos_h)


def prep(heads, tails, table, ints):
    cols = lambda dt: arr((D, E_DEV), dt)
    return call(
        prep_kernel, "prep", 1,
        [full((D, E_DEV)), full((D, E_DEV)), full((D, RELS)), full((1, INTS))],
        [full((D, E_DEV))] * 3 + [full((8, E_DEV))] + [full((1, E_DEV))] * 3 + [full((1, NEG_DEV)), full((U_CAP, LANES))],
        [cols(F32), cols(BF16), cols(BF16), arr((8, E_DEV), F32),
         arr((1, E_DEV), I32), arr((1, E_DEV), I32), arr((1, E_DEV), I32), arr((1, NEG_DEV), I32), arr((U_CAP, LANES), F32)],
        [pltpu.VMEM((D, REL_PAD), BF16)] * 3,
        mib=24,
    )(heads, tails, table, ints)


def edge_kernel(core_ref, n0_ref, n1_ref, n2_ref, n3_ref, head_ref, tail_ref, r_ref, q_ref, m_ref, pos_ref, rid_ref,
                pt_ref, ph_ref, dh_ref, dt_ref, mine_ref, other_ref, neg_ref, turned_ref):
    turn = eye(NEG_DEV)
    for k, ref in enumerate((n0_ref, n1_ref, n2_ref, n3_ref)):
        value = ref[...]
        neg_ref[:, pl.ds(k * NEG_DEV, NEG_DEV)] = value
        turned_ref[pl.ds(k * NEG_DEV, NEG_DEV), :] = dot_nt(turn, value).astype(BF16)

    head = head_ref[...].astype(F32)
    tail = tail_ref[...].astype(F32)
    firsts = []
    grads = []
    for side, (query_ref, positives, prob_ref) in enumerate(((q_ref, tail, pt_ref), (m_ref, head, ph_ref))):
        positive = pos_ref[pl.ds(side, 1), :]
        scores = dot(turned_ref[...], query_ref[...])
        top = jnp.maximum(positive, jnp.max(scores, 0, keepdims=True))
        weight = jnp.exp(scores - top)
        pos_weight = jnp.exp(positive - top)
        total = pos_weight + jnp.sum(weight, 0, keepdims=True)
        first = pos_weight / total - 1.0
        probs = (weight * (1.0 / total)).astype(BF16)
        prob_ref[...] = probs
        grads.append(first * positives + dot(neg_ref[...], probs))
        firsts.append(first)

    rel = r_ref[...]
    dq, dm = grads
    hr, hi, tr, ti, rr, ri = head[:HALF], head[HALF:], tail[:HALF], tail[HALF:], rel[:HALF], rel[HALF:]
    qr, qi, mr, mi = dq[:HALF], dq[HALF:], dm[:HALF], dm[HALF:]
    d_rel = jnp.concatenate([(hr * qr + hi * qi) + (tr * mr + ti * mi), (hr * qi - hi * qr) + (ti * mr - tr * mi)], 0)
    ids = rid_ref[...] - REL_HALF * core_ref[0]
    ids = jnp.where(ids < 0, ids + REL_PAD, ids)
    hit = one_hot(ids, REL_PAD)
    high, low = split2(d_rel)
    for ref, at in ((other_ref, REL_HALF), (mine_ref, 0)):
        part = hit[at:at + REL_HALF]
        ref[...] = (dot_nt(part, high) + dot_nt(part, low)).T

    d_head = firsts[1] * m_ref[...].astype(F32) + jnp.concatenate([rr * qr + ri * qi, rr * qi - ri * qr], 0)
    d_tail = firsts[0] * q_ref[...].astype(F32) + jnp.concatenate([rr * mr - ri * mi, rr * mi + ri * mr], 0)
    dh_ref[...] = d_head.astype(BF16)
    dt_ref[...] = d_tail.astype(BF16)


def edge(core, negs, h, t, r, q, m, pos, rid):
    part = (D, NEG_DEV)
    cols = (D, E_DEV)
    half = (D, REL_HALF)
    return call(
        edge_kernel, "edge", 1,
        [SMEM] + [full(part)] * 4 + [full(cols)] * 5 + [full((8, E_DEV)), full((1, E_DEV))],
        [full((NEG, E_DEV))] * 2 + [full(cols)] * 2 + [full(half)] * 2,
        [arr((NEG, E_DEV), BF16)] * 2 + [arr(cols, BF16)] * 2 + [arr(half, F32)] * 2,
        [pltpu.VMEM((D, NEG), BF16), pltpu.VMEM((NEG, D), BF16)],
        flops=10**10, mib=36,
    )(core, *negs, h, t, r, q, m, pos, rid)


def group_kernel(q_ref, m_ref, pt_ref, ph_ref, own_ref, g1_ref, g2_ref, g3_ref):
    term = dot_nt(q_ref[...], pt_ref[...]) + dot_nt(m_ref[...], ph_ref[...])
    own_ref[...] = term[:, :NEG_DEV]
    for k, ref in enumerate((g1_ref, g2_ref, g3_ref)):
        ref[...] = term[:, (k + 1) * NEG_DEV:(k + 2) * NEG_DEV].astype(BF16)


def group(q, m, pt, ph):
    part = (D, NEG_DEV)
    return call(
        group_kernel, "group", 1,
        [full((D, E_DEV))] * 2 + [full((NEG, E_DEV))] * 2, [full(part)] * 4, [arr(part, F32)] + [arr(part, BF16)] * 3,
        flops=4 * 10**9, mib=24,
    )(q, m, pt, ph)


def slot_kernel(target_h_ref, target_t_ref, dh_ref, dt_ref, code_ref, out_ref):
    hit_h = one_hot(target_h_ref[...], U_CAP)
    hit_t = one_hot(target_t_ref[...], U_CAP)
    total = dot_nt(hit_h, dh_ref[...]) + dot_nt(hit_t, dt_ref[...])
    code = code_ref[:, USED:]
    for k in range(N_GRP):
        out_ref[k] = jnp.concatenate([total[:, k * USED:(k + 1) * USED], code], 1)


def slot(th, tt, dh, dt, code):
    shape = (N_GRP, U_CAP, LANES)
    return call(
        slot_kernel, "slot", 1,
        [full((1, E_DEV))] * 2 + [full((D, E_DEV))] * 2 + [full((U_CAP, LANES))],
        full(shape), arr(shape, F32),
        flops=8 * 10**9, mib=24,
    )(th, tt, dh, dt, code)


def pack_kernel(target_ref, own_ref, g1_ref, g2_ref, g3_ref, part_ref, out_ref):
    rows = own_ref[...] + g1_ref[...].astype(F32) + g2_ref[...].astype(F32) + g3_ref[...].astype(F32)
    hit = one_hot(target_ref[...], U_CAP)
    rest = jnp.zeros((LANES - USED, NEG_DEV), F32)
    for k in range(N_GRP):
        high, low = split2(jnp.concatenate([rows[k * USED:(k + 1) * USED], rest], 0))
        out_ref[k] = (part_ref[k] + (dot_nt(hit, high) + dot_nt(hit, low))).astype(BF16)


def pack(tn, own, g1, g2, g3, part):
    shape = (N_GRP, U_CAP, LANES)
    return call(
        pack_kernel, "pack", 1,
        [full((1, NEG_DEV))] + [full((D, NEG_DEV))] * 4 + [full(shape)],
        full(shape), arr(shape, BF16),
        flops=3 * 10**9, mib=16,
    )(tn, own, g1, g2, g3, part)


def partition_kernel(rows_ref, out_ref, acc_ref):
    step = pl.program_id(0)
    rows = rows_ref[...]
    lane = lax.broadcasted_iota(I32, (8, LANES), 1)
    weight = jnp.where(lane == USED, 32.0, jnp.where(lane == USED + 1, 1.0, 0.0)).astype(BF16)
    ids = dot_nt(weight, rows)[:1].astype(I32)
    term = dot(one_hot(ids, ENT_DEV), rows)

    @pl.when(step == 0)
    def _():
        acc_ref[...] = term

    @pl.when(step > 0)
    def _():
        acc_ref[...] += term

    @pl.when(step == pl.num_programs(0) - 1)
    def _():
        out_ref[...] = acc_ref[...].T[:USED]


def partition(rows):
    block = rows.shape[0]
    return call(
        partition_kernel, "partition", rows.shape[0] // block,
        [pl.BlockSpec((block, LANES), lambda i: (i, 0))],
        full((USED, ENT_DEV)),
        arr((USED, ENT_DEV), F32),
        [pltpu.VMEM((ENT_DEV, LANES), F32)],
    )(rows)


def rel_chip_kernel(mine_ref, other_ref, out_ref):
    for k in range(REL_TILES):
        at = pl.ds(k * LANES, LANES)
        out_ref[pl.ds(k * D, D), :] = (mine_ref[:, at] + other_ref[:, at]).astype(BF16)
    rest = N_XY * REL_PART - REL_TILES * D
    out_ref[pl.ds(REL_TILES * D, rest), :] = jnp.zeros((rest, LANES), BF16)


def rel_chip(mine, other):
    shape = (N_XY * REL_PART, LANES)
    return call(rel_chip_kernel, "rel_chip", 1, [full((D, REL_HALF))] * 2, full(shape), arr(shape, BF16), mib=24)(mine, other)


def rel_xy_kernel(in_ref, out_ref):
    out_ref[...] = jnp.sum(in_ref[...].astype(F32), 0).astype(BF16)


def rel_xy(parts):
    shape = (REL_PART, LANES)
    return call(rel_xy_kernel, "rel_xy", 1, [full((N_XY,) + shape)], full(shape), arr(shape, BF16), mib=24)(parts)


def rel_z_kernel(*refs):
    values = [ref[...].astype(F32) for ref in refs[:-1]]
    while len(values) > 1:
        half = len(values) // 2
        values = [values[k] + values[k + half] for k in range(half)]
    refs[-1][...] = values[0].astype(BF16)


def rel_z(blocks):
    shape = (REL_PART, LANES)
    return call(rel_z_kernel, "rel_z", 1, [full(shape)] * 8, full(shape), arr(shape, BF16), mib=24, flops=3 * 10**10)(*blocks)


def place_kernel(me_ref, *refs):
    out_ref = refs[-1]
    rows = refs[0].shape[0]
    for k, ref in enumerate(refs[:-1]):
        at = pl.multiple_of(((me_ref[0] - k) & (N_GRP - 1)) * rows, rows)
        out_ref[pl.ds(at, rows), :] = ref[...]


def place(me, blocks, name):
    rows = blocks[0].shape[0]
    shape = (rows * N_GRP, LANES)
    return call(
        place_kernel, name, 1, [SMEM] + [full((rows, LANES))] * N_GRP, full(shape), arr(shape, BF16), mib=24
    )(me, *blocks)


def table_kernel(core_ref, mine_ref, other_ref, out_ref):
    for half, ref in enumerate((mine_ref, other_ref)):
        for place in range(2):
            @pl.when((core_ref[0] == half) == (place == 0))
            def _(ref=ref, place=place):
                for k in range(REL_TILES):
                    at = place * REL_HALF + k * LANES
                    width = min(LANES, RELS - at)
                    out_ref[:, pl.ds(at, width)] = ref[pl.ds(k * D, D), :].astype(F32)[:, :width]


def table(core, mine, other):
    return call(
        table_kernel, "table", 1, [SMEM] + [full((N_XY * REL_PART, LANES))] * 2, full((D, RELS)), arr((D, RELS), F32)
    )(core, mine, other)


def shift(value, axis, k, size=N_GRP):
    return lax.ppermute(value, axis, [(i, (i + k) % size) for i in range(size)])


def pair(value):
    return lax.ppermute(value, "c", [(0, 1), (1, 0)])


def around(value, axis):
    return [value] + [shift(value, axis, k) for k in (1, 2, 3)]


def shards(head_rows, tail_rows, rel_ids, neg_rows, rel_table, owner_counts, unique_ids, head_slot, tail_slot, negative_slot):
    core = lax.axis_index("c").astype(I32).reshape(1)
    x = lax.axis_index("x").astype(I32).reshape(1)
    y = lax.axis_index("y").astype(I32).reshape(1)
    heads, tails = head_rows.T, tail_rows.T
    negs = around(neg_rows.T, "x")
    ints = jnp.concatenate([
        rel_ids, head_slot, tail_slot, negative_slot, unique_ids[0], owner_counts[0],
        jnp.zeros((INTS - AT_COUNTS - N_OWN,), I32)]).reshape(1, INTS)
    r, q, m, pos, rid, th, tt, tn, code = prep(heads, tails, rel_table.T, ints)
    pt, ph, dh, dt, mine, other = edge(core, negs, heads, tails, r, q, m, pos, rid)
    own, g1, g2, g3 = group(q, m, pt, ph)
    back = [shift(g, "x", N_GRP - k) for k, g in ((1, g1), (2, g2), (3, g3))]
    other = pair(other)
    mine, other, own = lax.optimization_barrier((mine, other, own))
    chip = rel_chip(mine, other).reshape(N_XY, REL_PART, LANES)
    part = slot(th, tt, dh, dt, code)
    chip = lax.all_to_all(chip, ("x", "y"), 0, 0, tiled=True)
    packed = pack(tn, own, *back, part)
    chip, packed = lax.optimization_barrier((chip, packed))
    piece = rel_xy(chip)
    piece, packed = lax.optimization_barrier((piece, packed))
    piece = rel_z([piece] + [shift(piece, "z", k, 8) for k in range(1, 8)])
    received = lax.all_to_all(packed.reshape(N_GRP * N_OWN, CAP, LANES), ALL, 0, 0, tiled=True)
    quarter = place(y, around(piece, "y"), "place_y")
    half = place(x, around(quarter, "x"), "place_x")
    rel_grad = table(core, half, pair(half))
    entity_grad = partition(received.reshape(-1, LANES))
    return entity_grad.T, rel_grad.T


def solution(mesh):
    split = Mesh(mesh.devices.reshape(N_GRP, 4, 8, 2), ALL)
    edges = P(ALL)
    rows = P(ALL, None)
    in_specs = (rows, rows, edges, rows, P(), rows, rows, edges, edges, edges)
    out_specs = (P(("y", "z", "c"), "x"), P())
    return jax.shard_map(shards, mesh=split, in_specs=in_specs, out_specs=out_specs, check_vma=False)
```

```python
import jax
import jax.numpy as jnp
from jax import lax
from jax.experimental import pallas as pl
from jax.experimental.pallas import tpu as pltpu
from jax.sharding import Mesh
from jax.sharding import PartitionSpec as P

D = 400
HALF = D // 2
RELS = 1500
E_DEV = 768
ENT_DEV = 1024
NEG_DEV = 256
CAP = 16
NEG = 1024
U_CAP = 1024
N_GRP = 4
N_OWN = 64
N_XY = 16
LANES = 128
USED = D // N_GRP
REL_PAD = 1536
REL_HALF = REL_PAD // 2
REL_TILES = REL_HALF // 128
REL_PART = 160
AT_UID = 3 * E_DEV + NEG_DEV
AT_COUNTS = AT_UID + U_CAP
INTS = AT_COUNTS + 128
ALL = ("x", "y", "z", "c")
F32 = jnp.float32
BF16 = jnp.bfloat16
I32 = jnp.int32


def dot(a, b):
    return lax.dot_general(a, b, (((1,), (0,)), ((), ())), preferred_element_type=F32)


def dot_nt(a, b):
    return lax.dot_general(a, b, (((1,), (1,)), ((), ())), preferred_element_type=F32)


def split2(value):
    high = value.astype(BF16)
    return high, (value - high.astype(F32)).astype(BF16)


def eye(size):
    row = lax.broadcasted_iota(I32, (size, size), 0)
    col = lax.broadcasted_iota(I32, (size, size), 1)
    return jnp.where(row == col, 1.0, 0.0).astype(BF16)


def one_hot(ids_row, rows):
    spot = lax.broadcasted_iota(I32, (LANES, ids_row.shape[1]), 0).astype(BF16)
    blocks = []
    for at in range(0, rows, LANES):
        here = jnp.clip(ids_row - at, -1, LANES).astype(BF16)
        blocks.append(jnp.where(spot == here, jnp.ones((), BF16), jnp.zeros((), BF16)))
    return jnp.concatenate(blocks, 0)


def full(shape):
    return pl.BlockSpec(shape, lambda i: (0,) * len(shape))


def arr(shape, dtype):
    return jax.ShapeDtypeStruct(shape, dtype)


def call(kernel, name, grid, in_specs, out_specs, out_shape, scratch=(), mib=60, flops=10**6):
    return pl.pallas_call(
        kernel,
        name=name,
        grid=(grid,),
        in_specs=in_specs,
        out_specs=out_specs,
        out_shape=out_shape,
        scratch_shapes=list(scratch),
        compiler_params=pltpu.CompilerParams(vmem_limit_bytes=mib * 1024 * 1024),
        cost_estimate=pl.CostEstimate(flops=flops, bytes_accessed=10**5, transcendentals=0),
    )


SMEM = pl.BlockSpec(memory_space=pltpu.SMEM)


def prep_kernel(head_ref, tail_ref, table_ref, ints_ref,
                r_ref, q_ref, m_ref, pos_ref, rids_ref, th_ref, tt_ref, tn_ref, code_ref,
                high_ref, mid_ref, low_ref):
    table = table_ref[...]
    high = table.astype(BF16)
    rest = table - high.astype(F32)
    mid = rest.astype(BF16)
    low = (rest - mid.astype(F32)).astype(BF16)
    for ref, value in ((high_ref, high), (mid_ref, mid), (low_ref, low)):
        ref[:, pl.ds(REL_PAD - LANES, LANES)] = jnp.zeros((D, LANES), BF16)
        ref[:, pl.ds(0, RELS)] = value

    rids_ref[...] = ints_ref[:, :E_DEV]
    counts_row = ints_ref[:, AT_COUNTS:AT_COUNTS + N_OWN]
    counts = jnp.broadcast_to(counts_row, (N_OWN, N_OWN)).astype(F32)
    part = lax.broadcasted_iota(I32, (N_OWN, N_OWN), 0)
    other = lax.broadcasted_iota(I32, (N_OWN, N_OWN), 1)
    ends = jnp.sum(jnp.where(other <= part, counts, 0.0), 1, keepdims=True).astype(I32)
    own = jnp.sum(jnp.where(other == part, counts, 0.0), 1, keepdims=True).astype(I32)
    for out, at in ((th_ref, E_DEV), (tt_ref, 2 * E_DEV), (tn_ref, 3 * E_DEV)):
        slots = ints_ref[:, at:at + out.shape[1]]
        out[...] = slots + jnp.sum(jnp.where(slots >= ends, CAP - own, 0), 0, keepdims=True)

    place = lax.broadcasted_iota(I32, (U_CAP, N_OWN), 0)
    lane = (place & (CAP - 1)).astype(F32)
    owner = lax.broadcasted_iota(I32, (U_CAP, N_OWN), 1)
    counts_all = jnp.broadcast_to(counts_row, (U_CAP, N_OWN)).astype(F32)
    start = jnp.sum(jnp.where(owner < (place >> 4), counts_all, 0.0), 1, keepdims=True)
    count = jnp.sum(jnp.where(owner == (place >> 4), counts_all, 0.0), 1, keepdims=True)
    spot = (start + lane[:, :1]).astype(I32)
    column = lax.broadcasted_iota(I32, (U_CAP, U_CAP), 1)
    uid = ints_ref[:, AT_UID:AT_UID + U_CAP].astype(F32)
    picked = jnp.sum(jnp.where(column == spot, uid, 0.0), 1, keepdims=True)
    picked = jnp.where(lane[:, :1] < count, picked, float(ENT_DEV)).astype(I32)
    lanes = lax.broadcasted_iota(I32, (U_CAP, LANES), 1)
    code = jnp.where(lanes == USED, picked >> 5, jnp.where(lanes == USED + 1, picked & 31, 0))
    code_ref[...] = code.astype(F32)

    hit = one_hot(rids_ref[...], REL_PAD)
    rel = dot(high_ref[...], hit) + dot(mid_ref[...], hit) + dot(low_ref[...], hit)
    r_ref[...] = rel
    head = head_ref[...].astype(F32)
    tail = tail_ref[...].astype(F32)
    hr, hi, tr, ti, rr, ri = head[:HALF], head[HALF:], tail[:HALF], tail[HALF:], rel[:HALF], rel[HALF:]
    query = jnp.concatenate([hr * rr - hi * ri, hr * ri + hi * rr], 0).astype(BF16)
    mirror = jnp.concatenate([rr * tr + ri * ti, rr * ti - ri * tr], 0).astype(BF16)
    q_ref[...] = query
    m_ref[...] = mirror
    pos_t = jnp.sum(query.astype(F32) * tail, 0, keepdims=True)
    pos_h = jnp.sum(mirror.astype(F32) * head, 0, keepdims=True)
    side = lax.broadcasted_iota(I32, (8, E_DEV), 0)
    pos_ref[...] = jnp.where(side == 0, pos_t, pos_h)


def prep(heads, tails, table, ints):
    cols = lambda dt: arr((D, E_DEV), dt)
    return call(
        prep_kernel, "prep", 1,
        [full((D, E_DEV)), full((D, E_DEV)), full((D, RELS)), full((1, INTS))],
        [full((D, E_DEV))] * 3 + [full((8, E_DEV))] + [full((1, E_DEV))] * 3 + [full((1, NEG_DEV)), full((U_CAP, LANES))],
        [cols(F32), cols(BF16), cols(BF16), arr((8, E_DEV), F32),
         arr((1, E_DEV), I32), arr((1, E_DEV), I32), arr((1, E_DEV), I32), arr((1, NEG_DEV), I32), arr((U_CAP, LANES), F32)],
        [pltpu.VMEM((D, REL_PAD), BF16)] * 3,
        mib=24,
    )(heads, tails, table, ints)


def edge_kernel(core_ref, n0_ref, n1_ref, n2_ref, n3_ref, head_ref, tail_ref, r_ref, q_ref, m_ref, pos_ref, rid_ref,
                own_ref, g1_ref, g2_ref, g3_ref, rows_ref, mine_ref, other_ref, neg_ref, turned_ref):
    turn = eye(NEG_DEV)
    for k, ref in enumerate((n0_ref, n1_ref, n2_ref, n3_ref)):
        value = ref[...]
        neg_ref[:, pl.ds(k * NEG_DEV, NEG_DEV)] = value
        turned_ref[pl.ds(k * NEG_DEV, NEG_DEV), :] = dot_nt(turn, value).astype(BF16)

    head = head_ref[...].astype(F32)
    tail = tail_ref[...].astype(F32)
    firsts = []
    grads = []
    term = jnp.zeros((D, NEG), F32)
    for side, (query_ref, positives) in enumerate(((q_ref, tail), (m_ref, head))):
        positive = pos_ref[pl.ds(side, 1), :]
        scores = dot(turned_ref[...], query_ref[...])
        top = jnp.maximum(positive, jnp.max(scores, 0, keepdims=True))
        weight = jnp.exp(scores - top)
        pos_weight = jnp.exp(positive - top)
        total = pos_weight + jnp.sum(weight, 0, keepdims=True)
        first = pos_weight / total - 1.0
        probs = (weight * (1.0 / total)).astype(BF16)
        term = term + dot_nt(query_ref[...], probs)
        grads.append(first * positives + dot(neg_ref[...], probs))
        firsts.append(first)
    own_ref[...] = term[:, :NEG_DEV]
    for k, ref in enumerate((g1_ref, g2_ref, g3_ref)):
        ref[...] = term[:, (k + 1) * NEG_DEV:(k + 2) * NEG_DEV].astype(BF16)

    rel = r_ref[...]
    dq, dm = grads
    hr, hi, tr, ti, rr, ri = head[:HALF], head[HALF:], tail[:HALF], tail[HALF:], rel[:HALF], rel[HALF:]
    qr, qi, mr, mi = dq[:HALF], dq[HALF:], dm[:HALF], dm[HALF:]
    d_rel = jnp.concatenate([(hr * qr + hi * qi) + (tr * mr + ti * mi), (hr * qi - hi * qr) + (ti * mr - tr * mi)], 0)
    ids = rid_ref[...] - REL_HALF * core_ref[0]
    ids = jnp.where(ids < 0, ids + REL_PAD, ids)
    hit = one_hot(ids, REL_PAD)
    high, low = split2(d_rel)
    both = jnp.concatenate([high, low], 0)
    for ref, at in ((other_ref, REL_HALF), (mine_ref, 0)):
        term = dot_nt(both, hit[at:at + REL_HALF])
        ref[...] = term[:D] + term[D:]

    d_head = firsts[1] * m_ref[...].astype(F32) + jnp.concatenate([rr * qr + ri * qi, rr * qi - ri * qr], 0)
    d_tail = firsts[0] * q_ref[...].astype(F32) + jnp.concatenate([rr * mr - ri * mi, rr * mi + ri * mr], 0)
    rows_ref[:, pl.ds(0, E_DEV)] = d_head.astype(BF16)
    rows_ref[:, pl.ds(E_DEV, E_DEV)] = d_tail.astype(BF16)


def edge(core, negs, h, t, r, q, m, pos, rid):
    part = (D, NEG_DEV)
    cols = (D, E_DEV)
    half = (D, REL_HALF)
    return call(
        edge_kernel, "edge", 1,
        [SMEM] + [full(part)] * 4 + [full(cols)] * 5 + [full((8, E_DEV)), full((1, E_DEV))],
        [full(part)] * 4 + [full((D, 2 * E_DEV))] + [full(half)] * 2,
        [arr(part, F32)] + [arr(part, BF16)] * 3 + [arr((D, 2 * E_DEV), BF16)] + [arr(half, F32)] * 2,
        [pltpu.VMEM((D, NEG), BF16), pltpu.VMEM((NEG, D), BF16)],
        flops=10**10, mib=36,
    )(core, *negs, h, t, r, q, m, pos, rid)


def slot_kernel(target_h_ref, target_t_ref, rows_ref, code_ref, out_ref):
    hit_h = one_hot(target_h_ref[...], U_CAP)
    hit_t = one_hot(target_t_ref[...], U_CAP)
    total = dot_nt(hit_h, rows_ref[:, pl.ds(0, E_DEV)]) + dot_nt(hit_t, rows_ref[:, pl.ds(E_DEV, E_DEV)])
    code = code_ref[:, USED:]
    for k in range(N_GRP):
        out_ref[k] = jnp.concatenate([total[:, k * USED:(k + 1) * USED], code], 1)


def slot(th, tt, rows, code):
    shape = (N_GRP, U_CAP, LANES)
    return call(
        slot_kernel, "slot", 1,
        [full((1, E_DEV))] * 2 + [full((D, 2 * E_DEV)), full((U_CAP, LANES))],
        full(shape), arr(shape, F32),
        flops=8 * 10**9, mib=24,
    )(th, tt, rows, code)


def pack_kernel(target_ref, own_ref, g1_ref, g2_ref, g3_ref, part_ref, out_ref):
    rows = own_ref[...] + g1_ref[...].astype(F32) + g2_ref[...].astype(F32) + g3_ref[...].astype(F32)
    hit = one_hot(target_ref[...], U_CAP)
    rest = jnp.zeros((LANES - USED, NEG_DEV), F32)
    for k in range(N_GRP):
        high, low = split2(jnp.concatenate([rows[k * USED:(k + 1) * USED], rest], 0))
        out_ref[k] = (part_ref[k] + (dot_nt(hit, high) + dot_nt(hit, low))).astype(BF16)


def pack(tn, own, g1, g2, g3, part):
    shape = (N_GRP, U_CAP, LANES)
    return call(
        pack_kernel, "pack", 1,
        [full((1, NEG_DEV))] + [full((D, NEG_DEV))] * 4 + [full(shape)],
        full(shape), arr(shape, BF16),
        flops=3 * 10**9, mib=16,
    )(tn, own, g1, g2, g3, part)


def partition_kernel(rows_ref, out_ref, acc_ref):
    step = pl.program_id(0)
    rows = rows_ref[...]
    lane = lax.broadcasted_iota(I32, (8, LANES), 1)
    weight = jnp.where(lane == USED, 32.0, jnp.where(lane == USED + 1, 1.0, 0.0)).astype(BF16)
    ids = dot_nt(weight, rows)[:1].astype(I32)
    term = dot(one_hot(ids, ENT_DEV), rows)

    @pl.when(step == 0)
    def _():
        acc_ref[...] = term

    @pl.when(step > 0)
    def _():
        acc_ref[...] += term

    @pl.when(step == pl.num_programs(0) - 1)
    def _():
        out_ref[...] = acc_ref[...].T[:USED]


def partition(rows):
    block = rows.shape[0]
    return call(
        partition_kernel, "partition", rows.shape[0] // block,
        [pl.BlockSpec((block, LANES), lambda i: (i, 0))],
        full((USED, ENT_DEV)),
        arr((USED, ENT_DEV), F32),
        [pltpu.VMEM((ENT_DEV, LANES), F32)],
        mib=32,
    )(rows)


def rel_chip_kernel(mine_ref, other_ref, out_ref):
    for k in range(REL_TILES):
        at = pl.ds(k * LANES, LANES)
        out_ref[pl.ds(k * D, D), :] = (mine_ref[:, at] + other_ref[:, at]).astype(BF16)
    rest = N_XY * REL_PART - REL_TILES * D
    out_ref[pl.ds(REL_TILES * D, rest), :] = jnp.zeros((rest, LANES), BF16)


def rel_chip(mine, other):
    shape = (N_XY * REL_PART, LANES)
    return call(rel_chip_kernel, "rel_chip", 1, [full((D, REL_HALF))] * 2, full(shape), arr(shape, BF16), mib=12)(mine, other)


def rel_xy_kernel(in_ref, out_ref):
    out_ref[...] = jnp.sum(in_ref[...].astype(F32), 0).astype(BF16)


def rel_xy(parts):
    shape = (REL_PART, LANES)
    return call(rel_xy_kernel, "rel_xy", 1, [full((N_XY,) + shape)], full(shape), arr(shape, BF16), mib=12)(parts)


def chip_pair_kernel(core_ref, mine_ref, other_ref, out_ref):
    at = pl.multiple_of(core_ref[0] * REL_PART, REL_PART)
    out_ref[pl.ds(at, REL_PART), :] = mine_ref[...]
    out_ref[pl.ds(REL_PART - at, REL_PART), :] = other_ref[...]


def chip_pair(core, mine, other):
    shape = (REL_PART, LANES)
    out = (2 * REL_PART, LANES)
    return call(chip_pair_kernel, "chip_pair", 1, [SMEM] + [full(shape)] * 2, full(out), arr(out, BF16), mib=12)(core, mine, other)


def split_pair_kernel(core_ref, b1_ref, b2_ref, b3_ref, far_ref, mine_ref, other_ref):
    at = pl.multiple_of(core_ref[0] * REL_PART, REL_PART)
    for k, ref in enumerate((b1_ref, b2_ref, b3_ref)):
        mine_ref[pl.ds(k * REL_PART, REL_PART), :] = ref[pl.ds(at, REL_PART), :]
        other_ref[pl.ds(k * REL_PART, REL_PART), :] = ref[pl.ds(REL_PART - at, REL_PART), :]
    mine_ref[pl.ds(3 * REL_PART, REL_PART), :] = far_ref[...]


def split_pair(core, blocks, far):
    rows = (4 * REL_PART, LANES), (3 * REL_PART, LANES)
    return call(
        split_pair_kernel, "split_pair", 1, [SMEM] + [full((2 * REL_PART, LANES))] * 3 + [full((REL_PART, LANES))],
        [full(shape) for shape in rows], [arr(shape, BF16) for shape in rows], mib=12, flops=3 * 10**10
    )(core, *blocks, far)


def rel_z_kernel(core_ref, own_ref, mine_ref, other_ref, out_ref):
    value = lambda ref, k: ref[pl.ds(k * REL_PART, REL_PART), :].astype(F32)
    ahead = [value(mine_ref, k) for k in range(3)]
    behind = [value(other_ref, k) for k in range(3)]
    first = core_ref[0] == 0
    back = [own_ref[...].astype(F32)] + [jnp.where(first, a, b) for a, b in zip(ahead, behind)]
    back += [value(mine_ref, 3)] + [jnp.where(first, b, a) for a, b in zip(ahead[::-1], behind[::-1])]
    values = back
    while len(values) > 1:
        half = len(values) // 2
        values = [values[k] + values[k + half] for k in range(half)]
    out_ref[...] = values[0].astype(BF16)


def rel_z(core, own, mine, other):
    shape = (REL_PART, LANES)
    return call(
        rel_z_kernel, "rel_z", 1, [SMEM, full(shape), full((4 * REL_PART, LANES)), full((3 * REL_PART, LANES))], full(shape),
        arr(shape, BF16), mib=12,
    )(core, own, mine, other)


def place_kernel(me_ref, *refs):
    out_ref = refs[-1]
    rows = refs[0].shape[0]
    for k, ref in enumerate(refs[:-1]):
        at = pl.multiple_of(((me_ref[0] - k) & (N_GRP - 1)) * rows, rows)
        out_ref[pl.ds(at, rows), :] = ref[...]


def place(me, blocks, name):
    rows = blocks[0].shape[0]
    shape = (rows * N_GRP, LANES)
    return call(
        place_kernel, name, 1, [SMEM] + [full((rows, LANES))] * N_GRP, full(shape), arr(shape, BF16), mib=12
    )(me, *blocks)


def table_kernel(core_ref, mine_ref, other_ref, out_ref):
    for half, ref in enumerate((mine_ref, other_ref)):
        for place in range(2):
            @pl.when((core_ref[0] == half) == (place == 0))
            def _(ref=ref, place=place):
                for k in range(REL_TILES):
                    at = place * REL_HALF + k * LANES
                    width = min(LANES, RELS - at)
                    out_ref[:, pl.ds(at, width)] = ref[pl.ds(k * D, D), :].astype(F32)[:, :width]


def table(core, mine, other):
    return call(
        table_kernel, "table", 1, [SMEM] + [full((N_XY * REL_PART, LANES))] * 2, full((D, RELS)), arr((D, RELS), F32), mib=20
    )(core, mine, other)


def shift(value, axis, k, size=N_GRP):
    return lax.ppermute(value, axis, [(i, (i + k) % size) for i in range(size)])


def pair(value):
    return lax.ppermute(value, "c", [(0, 1), (1, 0)])


def shift_zc(value, ahead):
    pairs = [(2 * z + c, 2 * ((z + ahead[c]) % 8) + c) for z in range(8) for c in range(2)]
    return lax.ppermute(value, ("z", "c"), pairs)


def around(value, axis):
    return [value] + [shift(value, axis, k) for k in (1, 2, 3)]


def shards(head_rows, tail_rows, rel_ids, neg_rows, rel_table, owner_counts, unique_ids, head_slot, tail_slot, negative_slot):
    core = lax.axis_index("c").astype(I32).reshape(1)
    x = lax.axis_index("x").astype(I32).reshape(1)
    y = lax.axis_index("y").astype(I32).reshape(1)
    heads, tails = head_rows.T, tail_rows.T
    negs = around(neg_rows.T, "x")
    ints = jnp.concatenate([
        rel_ids, head_slot, tail_slot, negative_slot, unique_ids[0], owner_counts[0],
        jnp.zeros((INTS - AT_COUNTS - N_OWN,), I32)]).reshape(1, INTS)
    r, q, m, pos, rid, th, tt, tn, code = prep(heads, tails, rel_table.T, ints)
    own, g1, g2, g3, rows, mine, other = edge(core, negs, heads, tails, r, q, m, pos, rid)
    back = [shift(g, "x", N_GRP - k) for k, g in ((1, g1), (2, g2), (3, g3))]
    other = pair(other)
    chip = rel_chip(mine, other).reshape(N_XY, REL_PART, LANES)
    part = slot(th, tt, rows, code)
    chip = lax.all_to_all(chip, ("x", "y"), 0, 0, tiled=True)
    packed = pack(tn, own, *back, part)
    chip, packed = lax.optimization_barrier((chip, packed))
    piece = rel_xy(chip)
    piece, packed = lax.optimization_barrier((piece, packed))
    both = chip_pair(core, piece, pair(piece))
    mine, other = split_pair(core, [shift_zc(both, ahead) for ahead in ((1, 7), (2, 6), (3, 5))], shift(piece, "z", 4, 8))
    piece = rel_z(core, piece, mine, pair(other))
    received = lax.all_to_all(packed.reshape(N_GRP * N_OWN, CAP, LANES), ALL, 0, 0, tiled=True)
    quarter = place(y, around(piece, "y"), "place_y")
    half = place(x, around(quarter, "x"), "place_x")
    rel_grad = table(core, half, pair(half))
    entity_grad = partition(received.reshape(-1, LANES))
    return entity_grad.T, rel_grad.T


def solution(mesh):
    split = Mesh(mesh.devices.reshape(N_GRP, 4, 8, 2), ALL)
    edges = P(ALL)
    rows = P(ALL, None)
    in_specs = (rows, rows, edges, rows, P(), rows, rows, edges, edges, edges)
    out_specs = (P(("y", "z", "c"), "x"), P())
    return jax.shard_map(shards, mesh=split, in_specs=in_specs, out_specs=out_specs, check_vma=False)
```

```python
import jax
import jax.numpy as jnp
from jax import lax
from jax.experimental import pallas as pl
from jax.experimental.pallas import tpu as pltpu
from jax.sharding import Mesh
from jax.sharding import PartitionSpec as P

D = 400
HALF = D // 2
RELS = 1500
E_DEV = 768
ENT_DEV = 1024
NEG_DEV = 256
CAP = 16
NEG = 1024
U_CAP = 1024
N_GRP = 4
N_OWN = 64
N_XY = 16
LANES = 128
USED = D // N_GRP
REL_PAD = 1536
REL_HALF = REL_PAD // 2
REL_TILES = REL_HALF // 128
REL_PART = 160
AT_UID = 3 * E_DEV + NEG_DEV
AT_COUNTS = AT_UID + U_CAP
INTS = AT_COUNTS + 128
ALL = ("x", "y", "z", "c")
F32 = jnp.float32
BF16 = jnp.bfloat16
I32 = jnp.int32


def dot(a, b):
    return lax.dot_general(a, b, (((1,), (0,)), ((), ())), preferred_element_type=F32)


def dot_nt(a, b):
    return lax.dot_general(a, b, (((1,), (1,)), ((), ())), preferred_element_type=F32)


def split2(value):
    high = value.astype(BF16)
    return high, (value - high.astype(F32)).astype(BF16)


def eye(size):
    row = lax.broadcasted_iota(I32, (size, size), 0)
    col = lax.broadcasted_iota(I32, (size, size), 1)
    return jnp.where(row == col, 1.0, 0.0).astype(BF16)


def one_hot(ids_row, rows):
    spot = lax.broadcasted_iota(I32, (LANES, ids_row.shape[1]), 0).astype(BF16)
    blocks = []
    for at in range(0, rows, LANES):
        here = jnp.clip(ids_row - at, -1, LANES).astype(BF16)
        blocks.append(jnp.where(spot == here, jnp.ones((), BF16), jnp.zeros((), BF16)))
    return jnp.concatenate(blocks, 0)


def full(shape):
    return pl.BlockSpec(shape, lambda i: (0,) * len(shape))


def arr(shape, dtype):
    return jax.ShapeDtypeStruct(shape, dtype)


def call(kernel, name, grid, in_specs, out_specs, out_shape, scratch=(), mib=60, flops=10**6):
    return pl.pallas_call(
        kernel,
        name=name,
        grid=(grid,),
        in_specs=in_specs,
        out_specs=out_specs,
        out_shape=out_shape,
        scratch_shapes=list(scratch),
        compiler_params=pltpu.CompilerParams(vmem_limit_bytes=mib * 1024 * 1024),
        cost_estimate=pl.CostEstimate(flops=flops, bytes_accessed=10**5, transcendentals=0),
    )


SMEM = pl.BlockSpec(memory_space=pltpu.SMEM)


def prep_kernel(head_ref, tail_ref, table_ref, ints_ref,
                r_ref, q_ref, m_ref, pos_ref, rids_ref, th_ref, tt_ref, tn_ref, code_ref,
                high_ref, mid_ref, low_ref):
    table = table_ref[...]
    high = table.astype(BF16)
    rest = table - high.astype(F32)
    mid = rest.astype(BF16)
    low = (rest - mid.astype(F32)).astype(BF16)
    for ref, value in ((high_ref, high), (mid_ref, mid), (low_ref, low)):
        ref[:, pl.ds(REL_PAD - LANES, LANES)] = jnp.zeros((D, LANES), BF16)
        ref[:, pl.ds(0, RELS)] = value

    rids_ref[...] = ints_ref[:, :E_DEV]
    counts_row = ints_ref[:, AT_COUNTS:AT_COUNTS + N_OWN]
    counts = jnp.broadcast_to(counts_row, (N_OWN, N_OWN)).astype(F32)
    part = lax.broadcasted_iota(I32, (N_OWN, N_OWN), 0)
    other = lax.broadcasted_iota(I32, (N_OWN, N_OWN), 1)
    ends = jnp.sum(jnp.where(other <= part, counts, 0.0), 1, keepdims=True).astype(I32)
    own = jnp.sum(jnp.where(other == part, counts, 0.0), 1, keepdims=True).astype(I32)
    for out, at in ((th_ref, E_DEV), (tt_ref, 2 * E_DEV), (tn_ref, 3 * E_DEV)):
        slots = ints_ref[:, at:at + out.shape[1]]
        out[...] = slots + jnp.sum(jnp.where(slots >= ends, CAP - own, 0), 0, keepdims=True)

    place = lax.broadcasted_iota(I32, (U_CAP, N_OWN), 0)
    lane = (place & (CAP - 1)).astype(F32)
    owner = lax.broadcasted_iota(I32, (U_CAP, N_OWN), 1)
    counts_all = jnp.broadcast_to(counts_row, (U_CAP, N_OWN)).astype(F32)
    start = jnp.sum(jnp.where(owner < (place >> 4), counts_all, 0.0), 1, keepdims=True)
    count = jnp.sum(jnp.where(owner == (place >> 4), counts_all, 0.0), 1, keepdims=True)
    spot = (start + lane[:, :1]).astype(I32)
    column = lax.broadcasted_iota(I32, (U_CAP, U_CAP), 1)
    uid = ints_ref[:, AT_UID:AT_UID + U_CAP].astype(F32)
    picked = jnp.sum(jnp.where(column == spot, uid, 0.0), 1, keepdims=True)
    picked = jnp.where(lane[:, :1] < count, picked, float(ENT_DEV)).astype(I32)
    lanes = lax.broadcasted_iota(I32, (U_CAP, LANES), 1)
    code = jnp.where(lanes == USED, picked >> 5, jnp.where(lanes == USED + 1, picked & 31, 0))
    code_ref[...] = code.astype(F32)

    hit = one_hot(rids_ref[...], REL_PAD)
    rel = dot(high_ref[...], hit) + dot(mid_ref[...], hit) + dot(low_ref[...], hit)
    r_ref[...] = rel
    head = head_ref[...].astype(F32)
    tail = tail_ref[...].astype(F32)
    hr, hi, tr, ti, rr, ri = head[:HALF], head[HALF:], tail[:HALF], tail[HALF:], rel[:HALF], rel[HALF:]
    query = jnp.concatenate([hr * rr - hi * ri, hr * ri + hi * rr], 0).astype(BF16)
    mirror = jnp.concatenate([rr * tr + ri * ti, rr * ti - ri * tr], 0).astype(BF16)
    q_ref[...] = query
    m_ref[...] = mirror
    pos_t = jnp.sum(query.astype(F32) * tail, 0, keepdims=True)
    pos_h = jnp.sum(mirror.astype(F32) * head, 0, keepdims=True)
    side = lax.broadcasted_iota(I32, (8, E_DEV), 0)
    pos_ref[...] = jnp.where(side == 0, pos_t, pos_h)


def prep(heads, tails, table, ints):
    cols = lambda dt: arr((D, E_DEV), dt)
    return call(
        prep_kernel, "prep", 1,
        [full((D, E_DEV)), full((D, E_DEV)), full((D, RELS)), full((1, INTS))],
        [full((D, E_DEV))] * 3 + [full((8, E_DEV))] + [full((1, E_DEV))] * 3 + [full((1, NEG_DEV)), full((U_CAP, LANES))],
        [cols(F32), cols(BF16), cols(BF16), arr((8, E_DEV), F32),
         arr((1, E_DEV), I32), arr((1, E_DEV), I32), arr((1, E_DEV), I32), arr((1, NEG_DEV), I32), arr((U_CAP, LANES), F32)],
        [pltpu.VMEM((D, REL_PAD), BF16)] * 3,
        mib=24,
    )(heads, tails, table, ints)


def edge_kernel(core_ref, n0_ref, n1_ref, n2_ref, n3_ref, head_ref, tail_ref, r_ref, q_ref, m_ref, pos_ref, rid_ref,
                own_ref, g1_ref, g2_ref, g3_ref, rows_ref, mine_ref, other_ref, neg_ref, turned_ref):
    turn = eye(NEG_DEV)
    for k, ref in enumerate((n0_ref, n1_ref, n2_ref, n3_ref)):
        value = ref[...]
        neg_ref[:, pl.ds(k * NEG_DEV, NEG_DEV)] = value
        turned_ref[pl.ds(k * NEG_DEV, NEG_DEV), :] = dot_nt(turn, value).astype(BF16)

    head = head_ref[...].astype(F32)
    tail = tail_ref[...].astype(F32)
    firsts = []
    grads = []
    term = jnp.zeros((D, NEG), F32)
    for side, (query_ref, positives) in enumerate(((q_ref, tail), (m_ref, head))):
        positive = pos_ref[pl.ds(side, 1), :]
        scores = dot(turned_ref[...], query_ref[...])
        top = jnp.maximum(positive, jnp.max(scores, 0, keepdims=True))
        weight = jnp.exp(scores - top)
        pos_weight = jnp.exp(positive - top)
        total = pos_weight + jnp.sum(weight, 0, keepdims=True)
        first = pos_weight / total - 1.0
        probs = (weight * (1.0 / total)).astype(BF16)
        term = term + dot_nt(query_ref[...], probs)
        grads.append(first * positives + dot(neg_ref[...], probs))
        firsts.append(first)
    own_ref[...] = term[:, :NEG_DEV]
    for k, ref in enumerate((g1_ref, g2_ref, g3_ref)):
        ref[...] = term[:, (k + 1) * NEG_DEV:(k + 2) * NEG_DEV].astype(BF16)

    rel = r_ref[...]
    dq, dm = grads
    hr, hi, tr, ti, rr, ri = head[:HALF], head[HALF:], tail[:HALF], tail[HALF:], rel[:HALF], rel[HALF:]
    qr, qi, mr, mi = dq[:HALF], dq[HALF:], dm[:HALF], dm[HALF:]
    d_rel = jnp.concatenate([(hr * qr + hi * qi) + (tr * mr + ti * mi), (hr * qi - hi * qr) + (ti * mr - tr * mi)], 0)
    ids = rid_ref[...] - REL_HALF * core_ref[0]
    ids = jnp.where(ids < 0, ids + REL_PAD, ids)
    hit = one_hot(ids, REL_PAD)
    high, low = split2(d_rel)
    both = jnp.concatenate([high, low], 0)
    for ref, at in ((other_ref, REL_HALF), (mine_ref, 0)):
        term = dot_nt(both, hit[at:at + REL_HALF])
        ref[...] = term[:D] + term[D:]

    d_head = firsts[1] * m_ref[...].astype(F32) + jnp.concatenate([rr * qr + ri * qi, rr * qi - ri * qr], 0)
    d_tail = firsts[0] * q_ref[...].astype(F32) + jnp.concatenate([rr * mr - ri * mi, rr * mi + ri * mr], 0)
    for k, value in enumerate((d_head, d_tail)):
        high, low = split2(value)
        rows_ref[:, pl.ds(k * E_DEV, E_DEV)] = high
        rows_ref[:, pl.ds((k + 2) * E_DEV, E_DEV)] = low


def edge(core, negs, h, t, r, q, m, pos, rid):
    part = (D, NEG_DEV)
    cols = (D, E_DEV)
    half = (D, REL_HALF)
    return call(
        edge_kernel, "edge", 1,
        [SMEM] + [full(part)] * 4 + [full(cols)] * 5 + [full((8, E_DEV)), full((1, E_DEV))],
        [full(part)] * 4 + [full((D, 4 * E_DEV))] + [full(half)] * 2,
        [arr(part, F32)] + [arr(part, BF16)] * 3 + [arr((D, 4 * E_DEV), BF16)] + [arr(half, F32)] * 2,
        [pltpu.VMEM((D, NEG), BF16), pltpu.VMEM((NEG, D), BF16)],
        flops=10**10, mib=36,
    )(core, *negs, h, t, r, q, m, pos, rid)


def slot_kernel(target_h_ref, target_t_ref, rows_ref, code_ref, out_ref):
    hit_h = one_hot(target_h_ref[...], U_CAP)
    hit_t = one_hot(target_t_ref[...], U_CAP)
    parts = [rows_ref[:, pl.ds(k * E_DEV, E_DEV)] for k in range(4)]
    total = (dot_nt(hit_h, parts[0]) + dot_nt(hit_h, parts[2])) + (dot_nt(hit_t, parts[1]) + dot_nt(hit_t, parts[3]))
    code = code_ref[:, USED:]
    for k in range(N_GRP):
        out_ref[k] = jnp.concatenate([total[:, k * USED:(k + 1) * USED], code], 1)


def slot(th, tt, rows, code):
    shape = (N_GRP, U_CAP, LANES)
    return call(
        slot_kernel, "slot", 1,
        [full((1, E_DEV))] * 2 + [full((D, 4 * E_DEV)), full((U_CAP, LANES))],
        full(shape), arr(shape, F32),
        flops=8 * 10**9, mib=24,
    )(th, tt, rows, code)


def pack_kernel(target_ref, own_ref, g1_ref, g2_ref, g3_ref, part_ref, out_ref):
    rows = own_ref[...] + g1_ref[...].astype(F32) + g2_ref[...].astype(F32) + g3_ref[...].astype(F32)
    hit = one_hot(target_ref[...], U_CAP)
    rest = jnp.zeros((LANES - USED, NEG_DEV), F32)
    for k in range(N_GRP):
        high, low = split2(jnp.concatenate([rows[k * USED:(k + 1) * USED], rest], 0))
        out_ref[k] = (part_ref[k] + (dot_nt(hit, high) + dot_nt(hit, low))).astype(BF16)


def pack(tn, own, g1, g2, g3, part):
    shape = (N_GRP, U_CAP, LANES)
    return call(
        pack_kernel, "pack", 1,
        [full((1, NEG_DEV))] + [full((D, NEG_DEV))] * 4 + [full(shape)],
        full(shape), arr(shape, BF16),
        flops=3 * 10**9, mib=16,
    )(tn, own, g1, g2, g3, part)


def partition_kernel(rows_ref, out_ref, acc_ref):
    step = pl.program_id(0)
    rows = rows_ref[...]
    lane = lax.broadcasted_iota(I32, (8, LANES), 1)
    weight = jnp.where(lane == USED, 32.0, jnp.where(lane == USED + 1, 1.0, 0.0)).astype(BF16)
    ids = dot_nt(weight, rows)[:1].astype(I32)
    term = dot(one_hot(ids, ENT_DEV), rows)

    @pl.when(step == 0)
    def _():
        acc_ref[...] = term

    @pl.when(step > 0)
    def _():
        acc_ref[...] += term

    @pl.when(step == pl.num_programs(0) - 1)
    def _():
        out_ref[...] = acc_ref[...].T[:USED]


def partition(rows):
    block = rows.shape[0]
    return call(
        partition_kernel, "partition", rows.shape[0] // block,
        [pl.BlockSpec((block, LANES), lambda i: (i, 0))],
        full((USED, ENT_DEV)),
        arr((USED, ENT_DEV), F32),
        [pltpu.VMEM((ENT_DEV, LANES), F32)],
        mib=32,
    )(rows)


def rel_chip_kernel(mine_ref, other_ref, out_ref):
    for k in range(REL_TILES):
        at = pl.ds(k * LANES, LANES)
        out_ref[pl.ds(k * D, D), :] = (mine_ref[:, at] + other_ref[:, at]).astype(BF16)
    rest = N_XY * REL_PART - REL_TILES * D
    out_ref[pl.ds(REL_TILES * D, rest), :] = jnp.zeros((rest, LANES), BF16)


def rel_chip(mine, other):
    shape = (N_XY * REL_PART, LANES)
    return call(rel_chip_kernel, "rel_chip", 1, [full((D, REL_HALF))] * 2, full(shape), arr(shape, BF16), mib=12)(mine, other)


def rel_xy_kernel(in_ref, out_ref):
    out_ref[...] = jnp.sum(in_ref[...].astype(F32), 0).astype(BF16)


def rel_xy(parts):
    shape = (REL_PART, LANES)
    return call(rel_xy_kernel, "rel_xy", 1, [full((N_XY,) + shape)], full(shape), arr(shape, BF16), mib=12)(parts)


def chip_pair_kernel(core_ref, mine_ref, other_ref, out_ref):
    at = pl.multiple_of(core_ref[0] * REL_PART, REL_PART)
    out_ref[pl.ds(at, REL_PART), :] = mine_ref[...]
    out_ref[pl.ds(REL_PART - at, REL_PART), :] = other_ref[...]


def chip_pair(core, mine, other):
    shape = (REL_PART, LANES)
    out = (2 * REL_PART, LANES)
    return call(chip_pair_kernel, "chip_pair", 1, [SMEM] + [full(shape)] * 2, full(out), arr(out, BF16), mib=12)(core, mine, other)


def split_pair_kernel(core_ref, b1_ref, b2_ref, b3_ref, far_ref, mine_ref, other_ref):
    at = pl.multiple_of(core_ref[0] * REL_PART, REL_PART)
    for k, ref in enumerate((b1_ref, b2_ref, b3_ref)):
        mine_ref[pl.ds(k * REL_PART, REL_PART), :] = ref[pl.ds(at, REL_PART), :]
        other_ref[pl.ds(k * REL_PART, REL_PART), :] = ref[pl.ds(REL_PART - at, REL_PART), :]
    mine_ref[pl.ds(3 * REL_PART, REL_PART), :] = far_ref[...]


def split_pair(core, blocks, far):
    rows = (4 * REL_PART, LANES), (3 * REL_PART, LANES)
    return call(
        split_pair_kernel, "split_pair", 1, [SMEM] + [full((2 * REL_PART, LANES))] * 3 + [full((REL_PART, LANES))],
        [full(shape) for shape in rows], [arr(shape, BF16) for shape in rows], mib=12, flops=3 * 10**10
    )(core, *blocks, far)


def rel_z_kernel(core_ref, own_ref, mine_ref, other_ref, out_ref):
    value = lambda ref, k: ref[pl.ds(k * REL_PART, REL_PART), :].astype(F32)
    ahead = [value(mine_ref, k) for k in range(3)]
    behind = [value(other_ref, k) for k in range(3)]
    first = core_ref[0] == 0
    back = [own_ref[...].astype(F32)] + [jnp.where(first, a, b) for a, b in zip(ahead, behind)]
    back += [value(mine_ref, 3)] + [jnp.where(first, b, a) for a, b in zip(ahead[::-1], behind[::-1])]
    values = back
    while len(values) > 1:
        half = len(values) // 2
        values = [values[k] + values[k + half] for k in range(half)]
    out_ref[...] = values[0].astype(BF16)


def rel_z(core, own, mine, other):
    shape = (REL_PART, LANES)
    return call(
        rel_z_kernel, "rel_z", 1, [SMEM, full(shape), full((4 * REL_PART, LANES)), full((3 * REL_PART, LANES))], full(shape),
        arr(shape, BF16), mib=12,
    )(core, own, mine, other)


def place_kernel(me_ref, *refs):
    out_ref = refs[-1]
    rows = refs[0].shape[0]
    for k, ref in enumerate(refs[:-1]):
        at = pl.multiple_of(((me_ref[0] - k) & (N_GRP - 1)) * rows, rows)
        out_ref[pl.ds(at, rows), :] = ref[...]


def place(me, blocks, name):
    rows = blocks[0].shape[0]
    shape = (rows * N_GRP, LANES)
    return call(
        place_kernel, name, 1, [SMEM] + [full((rows, LANES))] * N_GRP, full(shape), arr(shape, BF16), mib=12
    )(me, *blocks)


def table_kernel(core_ref, mine_ref, other_ref, out_ref):
    for half, ref in enumerate((mine_ref, other_ref)):
        for place in range(2):
            @pl.when((core_ref[0] == half) == (place == 0))
            def _(ref=ref, place=place):
                for k in range(REL_TILES):
                    at = place * REL_HALF + k * LANES
                    width = min(LANES, RELS - at)
                    out_ref[:, pl.ds(at, width)] = ref[pl.ds(k * D, D), :].astype(F32)[:, :width]


def table(core, mine, other):
    return call(
        table_kernel, "table", 1, [SMEM] + [full((N_XY * REL_PART, LANES))] * 2, full((D, RELS)), arr((D, RELS), F32), mib=20
    )(core, mine, other)


def shift(value, axis, k, size=N_GRP):
    return lax.ppermute(value, axis, [(i, (i + k) % size) for i in range(size)])


def pair(value):
    return lax.ppermute(value, "c", [(0, 1), (1, 0)])


def shift_zc(value, ahead):
    pairs = [(2 * z + c, 2 * ((z + ahead[c]) % 8) + c) for z in range(8) for c in range(2)]
    return lax.ppermute(value, ("z", "c"), pairs)


def around(value, axis):
    return [value] + [shift(value, axis, k) for k in (1, 2, 3)]


def shards(head_rows, tail_rows, rel_ids, neg_rows, rel_table, owner_counts, unique_ids, head_slot, tail_slot, negative_slot):
    core = lax.axis_index("c").astype(I32).reshape(1)
    x = lax.axis_index("x").astype(I32).reshape(1)
    y = lax.axis_index("y").astype(I32).reshape(1)
    heads, tails = head_rows.T, tail_rows.T
    negs = around(neg_rows.T, "x")
    ints = jnp.concatenate([
        rel_ids, head_slot, tail_slot, negative_slot, unique_ids[0], owner_counts[0],
        jnp.zeros((INTS - AT_COUNTS - N_OWN,), I32)]).reshape(1, INTS)
    r, q, m, pos, rid, th, tt, tn, code = prep(heads, tails, rel_table.T, ints)
    own, g1, g2, g3, rows, mine, other = edge(core, negs, heads, tails, r, q, m, pos, rid)
    back = [shift(g, "x", N_GRP - k) for k, g in ((1, g1), (2, g2), (3, g3))]
    other = pair(other)
    chip = rel_chip(mine, other).reshape(N_XY, REL_PART, LANES)
    part = slot(th, tt, rows, code)
    chip = lax.all_to_all(chip, ("x", "y"), 0, 0, tiled=True)
    packed = pack(tn, own, *back, part)
    chip, packed = lax.optimization_barrier((chip, packed))
    piece = rel_xy(chip)
    piece, packed = lax.optimization_barrier((piece, packed))
    both = chip_pair(core, piece, pair(piece))
    mine, other = split_pair(core, [shift_zc(both, ahead) for ahead in ((1, 7), (2, 6), (3, 5))], shift(piece, "z", 4, 8))
    piece = rel_z(core, piece, mine, pair(other))
    received = lax.all_to_all(packed.reshape(N_GRP * N_OWN, CAP, LANES), ALL, 0, 0, tiled=True)
    quarter = place(y, around(piece, "y"), "place_y")
    half = place(x, around(quarter, "x"), "place_x")
    rel_grad = table(core, half, pair(half))
    entity_grad = partition(received.reshape(-1, LANES))
    return entity_grad.T, rel_grad.T


def solution(mesh):
    split = Mesh(mesh.devices.reshape(N_GRP, 4, 8, 2), ALL)
    edges = P(ALL)
    rows = P(ALL, None)
    in_specs = (rows, rows, edges, rows, P(), rows, rows, edges, edges, edges)
    out_specs = (P(("y", "z", "c"), "x"), P())
    return jax.shard_map(shards, mesh=split, in_specs=in_specs, out_specs=out_specs, check_vma=False)
```

```python
import jax
import jax.numpy as jnp
from jax import lax
from jax.experimental import pallas as pl
from jax.experimental.pallas import tpu as pltpu
from jax.sharding import Mesh
from jax.sharding import PartitionSpec as P

D = 400
HALF = D // 2
RELS = 1500
E_DEV = 768
ENT_DEV = 1024
NEG_DEV = 256
CAP = 16
NEG = 1024
U_CAP = 1024
N_GRP = 4
N_OWN = 64
N_XY = 16
LANES = 128
USED = D // N_GRP
REL_PAD = 1536
REL_HALF = REL_PAD // 2
REL_TILES = REL_HALF // 128
REL_PART = 160
AT_UID = 3 * E_DEV + NEG_DEV
AT_COUNTS = AT_UID + U_CAP
INTS = AT_COUNTS + 128
ALL = ("x", "y", "z", "c")
F32 = jnp.float32
BF16 = jnp.bfloat16
I32 = jnp.int32


def dot(a, b):
    return lax.dot_general(a, b, (((1,), (0,)), ((), ())), preferred_element_type=F32)


def dot_nt(a, b):
    return lax.dot_general(a, b, (((1,), (1,)), ((), ())), preferred_element_type=F32)


def split2(value):
    high = value.astype(BF16)
    return high, (value - high.astype(F32)).astype(BF16)


def eye(size):
    row = lax.broadcasted_iota(I32, (size, size), 0)
    col = lax.broadcasted_iota(I32, (size, size), 1)
    return jnp.where(row == col, 1.0, 0.0).astype(BF16)


def one_hot(ids_row, rows):
    spot = lax.broadcasted_iota(I32, (LANES, ids_row.shape[1]), 0).astype(BF16)
    blocks = []
    for at in range(0, rows, LANES):
        here = jnp.clip(ids_row - at, -1, LANES).astype(BF16)
        blocks.append(jnp.where(spot == here, jnp.ones((), BF16), jnp.zeros((), BF16)))
    return jnp.concatenate(blocks, 0)


def full(shape):
    return pl.BlockSpec(shape, lambda i: (0,) * len(shape))


def arr(shape, dtype):
    return jax.ShapeDtypeStruct(shape, dtype)


def call(kernel, name, grid, in_specs, out_specs, out_shape, scratch=(), mib=60, flops=10**6):
    return pl.pallas_call(
        kernel,
        name=name,
        grid=(grid,),
        in_specs=in_specs,
        out_specs=out_specs,
        out_shape=out_shape,
        scratch_shapes=list(scratch),
        compiler_params=pltpu.CompilerParams(vmem_limit_bytes=mib * 1024 * 1024),
        cost_estimate=pl.CostEstimate(flops=flops, bytes_accessed=10**5, transcendentals=0),
    )


SMEM = pl.BlockSpec(memory_space=pltpu.SMEM)


def prep_kernel(head_ref, tail_ref, table_ref, ints_ref,
                r_ref, q_ref, m_ref, pos_ref, rids_ref, th_ref, tt_ref, tn_ref, code_ref,
                high_ref, mid_ref, low_ref):
    table = table_ref[...]
    high = table.astype(BF16)
    rest = table - high.astype(F32)
    mid = rest.astype(BF16)
    low = (rest - mid.astype(F32)).astype(BF16)
    for ref, value in ((high_ref, high), (mid_ref, mid), (low_ref, low)):
        ref[:, pl.ds(REL_PAD - LANES, LANES)] = jnp.zeros((D, LANES), BF16)
        ref[:, pl.ds(0, RELS)] = value

    rids_ref[...] = ints_ref[:, :E_DEV]
    counts_row = ints_ref[:, AT_COUNTS:AT_COUNTS + N_OWN]
    counts = jnp.broadcast_to(counts_row, (N_OWN, N_OWN)).astype(F32)
    part = lax.broadcasted_iota(I32, (N_OWN, N_OWN), 0)
    other = lax.broadcasted_iota(I32, (N_OWN, N_OWN), 1)
    ends = jnp.sum(jnp.where(other <= part, counts, 0.0), 1, keepdims=True).astype(I32)
    own = jnp.sum(jnp.where(other == part, counts, 0.0), 1, keepdims=True).astype(I32)
    for out, at in ((th_ref, E_DEV), (tt_ref, 2 * E_DEV), (tn_ref, 3 * E_DEV)):
        slots = ints_ref[:, at:at + out.shape[1]]
        out[...] = slots + jnp.sum(jnp.where(slots >= ends, CAP - own, 0), 0, keepdims=True)

    place = lax.broadcasted_iota(I32, (U_CAP, N_OWN), 0)
    lane = (place & (CAP - 1)).astype(F32)
    owner = lax.broadcasted_iota(I32, (U_CAP, N_OWN), 1)
    counts_all = jnp.broadcast_to(counts_row, (U_CAP, N_OWN)).astype(F32)
    start = jnp.sum(jnp.where(owner < (place >> 4), counts_all, 0.0), 1, keepdims=True)
    count = jnp.sum(jnp.where(owner == (place >> 4), counts_all, 0.0), 1, keepdims=True)
    spot = (start + lane[:, :1]).astype(I32)
    column = lax.broadcasted_iota(I32, (U_CAP, U_CAP), 1)
    uid = ints_ref[:, AT_UID:AT_UID + U_CAP].astype(F32)
    picked = jnp.sum(jnp.where(column == spot, uid, 0.0), 1, keepdims=True)
    picked = jnp.where(lane[:, :1] < count, picked, float(ENT_DEV)).astype(I32)
    lanes = lax.broadcasted_iota(I32, (U_CAP, LANES), 1)
    code = jnp.where(lanes == USED, picked >> 5, jnp.where(lanes == USED + 1, picked & 31, 0))
    code_ref[...] = code.astype(F32)

    hit = one_hot(rids_ref[...], REL_PAD)
    rel = dot(high_ref[...], hit) + dot(mid_ref[...], hit) + dot(low_ref[...], hit)
    r_ref[...] = rel
    head = head_ref[...].astype(F32)
    tail = tail_ref[...].astype(F32)
    hr, hi, tr, ti, rr, ri = head[:HALF], head[HALF:], tail[:HALF], tail[HALF:], rel[:HALF], rel[HALF:]
    query = jnp.concatenate([hr * rr - hi * ri, hr * ri + hi * rr], 0).astype(BF16)
    mirror = jnp.concatenate([rr * tr + ri * ti, rr * ti - ri * tr], 0).astype(BF16)
    q_ref[...] = query
    m_ref[...] = mirror
    pos_t = jnp.sum(query.astype(F32) * tail, 0, keepdims=True)
    pos_h = jnp.sum(mirror.astype(F32) * head, 0, keepdims=True)
    side = lax.broadcasted_iota(I32, (8, E_DEV), 0)
    pos_ref[...] = jnp.where(side == 0, pos_t, pos_h)


def prep(heads, tails, table, ints):
    cols = lambda dt: arr((D, E_DEV), dt)
    return call(
        prep_kernel, "prep", 1,
        [full((D, E_DEV)), full((D, E_DEV)), full((D, RELS)), full((1, INTS))],
        [full((D, E_DEV))] * 3 + [full((8, E_DEV))] + [full((1, E_DEV))] * 3 + [full((1, NEG_DEV)), full((U_CAP, LANES))],
        [cols(F32), cols(BF16), cols(BF16), arr((8, E_DEV), F32),
         arr((1, E_DEV), I32), arr((1, E_DEV), I32), arr((1, E_DEV), I32), arr((1, NEG_DEV), I32), arr((U_CAP, LANES), F32)],
        [pltpu.VMEM((D, REL_PAD), BF16)] * 3,
        mib=24,
    )(heads, tails, table, ints)


def edge_kernel(core_ref, n0_ref, n1_ref, n2_ref, n3_ref, head_ref, tail_ref, r_ref, q_ref, m_ref, pos_ref, rid_ref,
                own_ref, g1_ref, g2_ref, g3_ref, rows_ref, mine_ref, other_ref, neg_ref, turned_ref):
    turn = eye(NEG_DEV)
    for k, ref in enumerate((n0_ref, n1_ref, n2_ref, n3_ref)):
        value = ref[...]
        neg_ref[:, pl.ds(k * NEG_DEV, NEG_DEV)] = value
        turned_ref[pl.ds(k * NEG_DEV, NEG_DEV), :] = dot_nt(turn, value).astype(BF16)

    head = head_ref[...].astype(F32)
    tail = tail_ref[...].astype(F32)
    firsts = []
    grads = []
    term = jnp.zeros((D, NEG), F32)
    for side, (query_ref, positives) in enumerate(((q_ref, tail), (m_ref, head))):
        positive = pos_ref[pl.ds(side, 1), :]
        scores = dot(turned_ref[...], query_ref[...])
        top = jnp.maximum(positive, jnp.max(scores, 0, keepdims=True))
        weight = jnp.exp(scores - top)
        pos_weight = jnp.exp(positive - top)
        total = pos_weight + jnp.sum(weight, 0, keepdims=True)
        first = pos_weight / total - 1.0
        probs = (weight * (1.0 / total)).astype(BF16)
        term = term + dot_nt(query_ref[...], probs)
        grads.append(first * positives + dot(neg_ref[...], probs))
        firsts.append(first)
    own_ref[...] = term[:, :NEG_DEV]
    for k, ref in enumerate((g1_ref, g2_ref, g3_ref)):
        ref[...] = term[:, (k + 1) * NEG_DEV:(k + 2) * NEG_DEV].astype(BF16)

    rel = r_ref[...]
    dq, dm = grads
    hr, hi, tr, ti, rr, ri = head[:HALF], head[HALF:], tail[:HALF], tail[HALF:], rel[:HALF], rel[HALF:]
    qr, qi, mr, mi = dq[:HALF], dq[HALF:], dm[:HALF], dm[HALF:]
    d_rel = jnp.concatenate([(hr * qr + hi * qi) + (tr * mr + ti * mi), (hr * qi - hi * qr) + (ti * mr - tr * mi)], 0)
    ids = rid_ref[...] - REL_HALF * core_ref[0]
    ids = jnp.where(ids < 0, ids + REL_PAD, ids)
    hit = one_hot(ids, REL_PAD)
    high, low = split2(d_rel)
    both = jnp.concatenate([high, low], 0)
    for ref, at in ((other_ref, REL_HALF), (mine_ref, 0)):
        term = dot_nt(both, hit[at:at + REL_HALF])
        ref[...] = term[:D] + term[D:]

    d_head = firsts[1] * m_ref[...].astype(F32) + jnp.concatenate([rr * qr + ri * qi, rr * qi - ri * qr], 0)
    d_tail = firsts[0] * q_ref[...].astype(F32) + jnp.concatenate([rr * mr - ri * mi, rr * mi + ri * mr], 0)
    for k, value in enumerate((d_head, d_tail)):
        high, low = split2(value)
        rows_ref[:, pl.ds(k * E_DEV, E_DEV)] = high
        rows_ref[:, pl.ds((k + 2) * E_DEV, E_DEV)] = low


def edge(core, negs, h, t, r, q, m, pos, rid):
    part = (D, NEG_DEV)
    cols = (D, E_DEV)
    half = (D, REL_HALF)
    return call(
        edge_kernel, "edge", 1,
        [SMEM] + [full(part)] * 4 + [full(cols)] * 5 + [full((8, E_DEV)), full((1, E_DEV))],
        [full(part)] * 4 + [full((D, 4 * E_DEV))] + [full(half)] * 2,
        [arr(part, F32)] + [arr(part, BF16)] * 3 + [arr((D, 4 * E_DEV), BF16)] + [arr(half, F32)] * 2,
        [pltpu.VMEM((D, NEG), BF16), pltpu.VMEM((NEG, D), BF16)],
        flops=10**10, mib=36,
    )(core, *negs, h, t, r, q, m, pos, rid)


def slot_kernel(target_h_ref, target_t_ref, rows_ref, code_ref, out_ref):
    hit_h = one_hot(target_h_ref[...], U_CAP)
    hit_t = one_hot(target_t_ref[...], U_CAP)
    parts = [rows_ref[:, pl.ds(k * E_DEV, E_DEV)] for k in range(4)]
    total = (dot_nt(hit_h, parts[0]) + dot_nt(hit_h, parts[2])) + (dot_nt(hit_t, parts[1]) + dot_nt(hit_t, parts[3]))
    code = code_ref[:, USED:]
    for k in range(N_GRP):
        out_ref[k] = jnp.concatenate([total[:, k * USED:(k + 1) * USED], code], 1)


def slot(th, tt, rows, code):
    shape = (N_GRP, U_CAP, LANES)
    return call(
        slot_kernel, "slot", 1,
        [full((1, E_DEV))] * 2 + [full((D, 4 * E_DEV)), full((U_CAP, LANES))],
        full(shape), arr(shape, F32),
        flops=8 * 10**9, mib=24,
    )(th, tt, rows, code)


def pack_kernel(target_ref, own_ref, g1_ref, g2_ref, g3_ref, part_ref, out_ref):
    rows = own_ref[...] + g1_ref[...].astype(F32) + g2_ref[...].astype(F32) + g3_ref[...].astype(F32)
    hit = one_hot(target_ref[...], U_CAP)
    rest = jnp.zeros((LANES - USED, NEG_DEV), F32)
    for k in range(N_GRP):
        high, low = split2(jnp.concatenate([rows[k * USED:(k + 1) * USED], rest], 0))
        out_ref[k] = (part_ref[k] + (dot_nt(hit, high) + dot_nt(hit, low))).astype(BF16)


def pack(tn, own, g1, g2, g3, part):
    shape = (N_GRP, U_CAP, LANES)
    return call(
        pack_kernel, "pack", 1,
        [full((1, NEG_DEV))] + [full((D, NEG_DEV))] * 4 + [full(shape)],
        full(shape), arr(shape, BF16),
        flops=3 * 10**9, mib=16,
    )(tn, own, g1, g2, g3, part)


def partition_kernel(rows_ref, out_ref, acc_ref):
    step = pl.program_id(0)
    rows = rows_ref[...]
    lane = lax.broadcasted_iota(I32, (8, LANES), 1)
    weight = jnp.where(lane == USED, 32.0, jnp.where(lane == USED + 1, 1.0, 0.0)).astype(BF16)
    ids = dot_nt(weight, rows)[:1].astype(I32)
    group = jnp.broadcast_to(rows[:, USED:USED + 1], rows.shape)
    none = jnp.zeros((), BF16)
    lower = jnp.where(group < 16, rows, none)
    upper = jnp.where(group < 32, rows, none) - lower
    both = dot(one_hot(ids & (ENT_DEV // 2 - 1), ENT_DEV // 2), jnp.concatenate([lower, upper], 1))
    term = jnp.concatenate([both[:, :LANES], both[:, LANES:]], 0)

    @pl.when(step == 0)
    def _():
        acc_ref[...] = term

    @pl.when(step > 0)
    def _():
        acc_ref[...] += term

    @pl.when(step == pl.num_programs(0) - 1)
    def _():
        out_ref[...] = acc_ref[...].T[:USED]


def partition(rows):
    block = rows.shape[0]
    return call(
        partition_kernel, "partition", rows.shape[0] // block,
        [pl.BlockSpec((block, LANES), lambda i: (i, 0))],
        full((USED, ENT_DEV)),
        arr((USED, ENT_DEV), F32),
        [pltpu.VMEM((ENT_DEV, LANES), F32)],
        mib=32,
    )(rows)


def rel_chip_kernel(mine_ref, other_ref, out_ref):
    for k in range(REL_TILES):
        at = pl.ds(k * LANES, LANES)
        out_ref[pl.ds(k * D, D), :] = (mine_ref[:, at] + other_ref[:, at]).astype(BF16)
    rest = N_XY * REL_PART - REL_TILES * D
    out_ref[pl.ds(REL_TILES * D, rest), :] = jnp.zeros((rest, LANES), BF16)


def rel_chip(mine, other):
    shape = (N_XY * REL_PART, LANES)
    return call(rel_chip_kernel, "rel_chip", 1, [full((D, REL_HALF))] * 2, full(shape), arr(shape, BF16), mib=12)(mine, other)


def rel_xy_kernel(in_ref, out_ref):
    out_ref[...] = jnp.sum(in_ref[...].astype(F32), 0).astype(BF16)


def rel_xy(parts):
    shape = (REL_PART, LANES)
    return call(rel_xy_kernel, "rel_xy", 1, [full((N_XY,) + shape)], full(shape), arr(shape, BF16), mib=12)(parts)


def chip_pair_kernel(core_ref, mine_ref, other_ref, out_ref):
    at = pl.multiple_of(core_ref[0] * REL_PART, REL_PART)
    out_ref[pl.ds(at, REL_PART), :] = mine_ref[...]
    out_ref[pl.ds(REL_PART - at, REL_PART), :] = other_ref[...]


def chip_pair(core, mine, other):
    shape = (REL_PART, LANES)
    out = (2 * REL_PART, LANES)
    return call(chip_pair_kernel, "chip_pair", 1, [SMEM] + [full(shape)] * 2, full(out), arr(out, BF16), mib=12)(core, mine, other)


def split_pair_kernel(core_ref, b1_ref, b2_ref, b3_ref, far_ref, mine_ref, other_ref):
    at = pl.multiple_of(core_ref[0] * REL_PART, REL_PART)
    for k, ref in enumerate((b1_ref, b2_ref, b3_ref)):
        mine_ref[pl.ds(k * REL_PART, REL_PART), :] = ref[pl.ds(at, REL_PART), :]
        other_ref[pl.ds(k * REL_PART, REL_PART), :] = ref[pl.ds(REL_PART - at, REL_PART), :]
    mine_ref[pl.ds(3 * REL_PART, REL_PART), :] = far_ref[...]


def split_pair(core, blocks, far):
    rows = (4 * REL_PART, LANES), (3 * REL_PART, LANES)
    return call(
        split_pair_kernel, "split_pair", 1, [SMEM] + [full((2 * REL_PART, LANES))] * 3 + [full((REL_PART, LANES))],
        [full(shape) for shape in rows], [arr(shape, BF16) for shape in rows], mib=12, flops=3 * 10**10
    )(core, *blocks, far)


def rel_z_kernel(core_ref, own_ref, mine_ref, other_ref, out_ref):
    value = lambda ref, k: ref[pl.ds(k * REL_PART, REL_PART), :].astype(F32)
    ahead = [value(mine_ref, k) for k in range(3)]
    behind = [value(other_ref, k) for k in range(3)]
    first = core_ref[0] == 0
    back = [own_ref[...].astype(F32)] + [jnp.where(first, a, b) for a, b in zip(ahead, behind)]
    back += [value(mine_ref, 3)] + [jnp.where(first, b, a) for a, b in zip(ahead[::-1], behind[::-1])]
    values = back
    while len(values) > 1:
        half = len(values) // 2
        values = [values[k] + values[k + half] for k in range(half)]
    out_ref[...] = values[0].astype(BF16)


def rel_z(core, own, mine, other):
    shape = (REL_PART, LANES)
    return call(
        rel_z_kernel, "rel_z", 1, [SMEM, full(shape), full((4 * REL_PART, LANES)), full((3 * REL_PART, LANES))], full(shape),
        arr(shape, BF16), mib=12,
    )(core, own, mine, other)


def place_kernel(me_ref, *refs):
    out_ref = refs[-1]
    rows = refs[0].shape[0]
    for k, ref in enumerate(refs[:-1]):
        at = pl.multiple_of(((me_ref[0] - k) & (N_GRP - 1)) * rows, rows)
        out_ref[pl.ds(at, rows), :] = ref[...]


def place(me, blocks, name):
    rows = blocks[0].shape[0]
    shape = (rows * N_GRP, LANES)
    return call(
        place_kernel, name, 1, [SMEM] + [full((rows, LANES))] * N_GRP, full(shape), arr(shape, BF16), mib=12
    )(me, *blocks)


def table_kernel(core_ref, mine_ref, other_ref, out_ref):
    for half, ref in enumerate((mine_ref, other_ref)):
        for place in range(2):
            @pl.when((core_ref[0] == half) == (place == 0))
            def _(ref=ref, place=place):
                for k in range(REL_TILES):
                    at = place * REL_HALF + k * LANES
                    width = min(LANES, RELS - at)
                    out_ref[:, pl.ds(at, width)] = ref[pl.ds(k * D, D), :].astype(F32)[:, :width]


def table(core, mine, other):
    return call(
        table_kernel, "table", 1, [SMEM] + [full((N_XY * REL_PART, LANES))] * 2, full((D, RELS)), arr((D, RELS), F32), mib=20
    )(core, mine, other)


def shift(value, axis, k, size=N_GRP):
    return lax.ppermute(value, axis, [(i, (i + k) % size) for i in range(size)])


def pair(value):
    return lax.ppermute(value, "c", [(0, 1), (1, 0)])


def shift_zc(value, ahead):
    pairs = [(2 * z + c, 2 * ((z + ahead[c]) % 8) + c) for z in range(8) for c in range(2)]
    return lax.ppermute(value, ("z", "c"), pairs)


def around(value, axis):
    return [value] + [shift(value, axis, k) for k in (1, 2, 3)]


def shards(head_rows, tail_rows, rel_ids, neg_rows, rel_table, owner_counts, unique_ids, head_slot, tail_slot, negative_slot):
    core = lax.axis_index("c").astype(I32).reshape(1)
    x = lax.axis_index("x").astype(I32).reshape(1)
    y = lax.axis_index("y").astype(I32).reshape(1)
    heads, tails = head_rows.T, tail_rows.T
    negs = around(neg_rows.T, "x")
    ints = jnp.concatenate([
        rel_ids, head_slot, tail_slot, negative_slot, unique_ids[0], owner_counts[0],
        jnp.zeros((INTS - AT_COUNTS - N_OWN,), I32)]).reshape(1, INTS)
    r, q, m, pos, rid, th, tt, tn, code = prep(heads, tails, rel_table.T, ints)
    own, g1, g2, g3, rows, mine, other = edge(core, negs, heads, tails, r, q, m, pos, rid)
    back = [shift(g, "x", N_GRP - k) for k, g in ((1, g1), (2, g2), (3, g3))]
    other = pair(other)
    chip = rel_chip(mine, other).reshape(N_XY, REL_PART, LANES)
    part = slot(th, tt, rows, code)
    chip = lax.all_to_all(chip, ("x", "y"), 0, 0, tiled=True)
    packed = pack(tn, own, *back, part)
    chip, packed = lax.optimization_barrier((chip, packed))
    piece = rel_xy(chip)
    piece, packed = lax.optimization_barrier((piece, packed))
    both = chip_pair(core, piece, pair(piece))
    mine, other = split_pair(core, [shift_zc(both, ahead) for ahead in ((1, 7), (2, 6), (3, 5))], shift(piece, "z", 4, 8))
    piece = rel_z(core, piece, mine, pair(other))
    received = lax.all_to_all(packed.reshape(N_GRP * N_OWN, CAP, LANES), ALL, 0, 0, tiled=True)
    quarter = place(y, around(piece, "y"), "place_y")
    half = place(x, around(quarter, "x"), "place_x")
    rel_grad = table(core, half, pair(half))
    entity_grad = partition(received.reshape(-1, LANES))
    return entity_grad.T, rel_grad.T


def solution(mesh):
    split = Mesh(mesh.devices.reshape(N_GRP, 4, 8, 2), ALL)
    edges = P(ALL)
    rows = P(ALL, None)
    in_specs = (rows, rows, edges, rows, P(), rows, rows, edges, edges, edges)
    out_specs = (P(("y", "z", "c"), "x"), P())
    return jax.shard_map(shards, mesh=split, in_specs=in_specs, out_specs=out_specs, check_vma=False)
```

```python
import jax
import jax.numpy as jnp
from jax import lax
from jax.experimental import pallas as pl
from jax.experimental.pallas import tpu as pltpu
from jax.sharding import Mesh
from jax.sharding import PartitionSpec as P

D = 400
HALF = D // 2
RELS = 1500
E_DEV = 768
ENT_DEV = 1024
NEG_DEV = 256
CAP = 16
NEG = 1024
U_CAP = 1024
N_GRP = 4
N_OWN = 64
N_XY = 16
LANES = 128
USED = D // N_GRP
REL_PAD = 1536
REL_HALF = REL_PAD // 2
REL_TILES = REL_HALF // 128
REL_PART = 160
AT_UID = 3 * E_DEV + NEG_DEV
AT_COUNTS = AT_UID + U_CAP
INTS = AT_COUNTS + 128
ALL = ("x", "y", "z", "c")
F32 = jnp.float32
BF16 = jnp.bfloat16
I32 = jnp.int32


def dot(a, b):
    return lax.dot_general(a, b, (((1,), (0,)), ((), ())), preferred_element_type=F32)


def dot_nt(a, b):
    return lax.dot_general(a, b, (((1,), (1,)), ((), ())), preferred_element_type=F32)


def split2(value):
    high = value.astype(BF16)
    return high, (value - high.astype(F32)).astype(BF16)


def eye(size):
    row = lax.broadcasted_iota(I32, (size, size), 0)
    col = lax.broadcasted_iota(I32, (size, size), 1)
    return jnp.where(row == col, 1.0, 0.0).astype(BF16)


def one_hot(ids_row, rows):
    spot = lax.broadcasted_iota(I32, (LANES, ids_row.shape[1]), 0).astype(BF16)
    blocks = []
    for at in range(0, rows, LANES):
        here = jnp.clip(ids_row - at, -1, LANES).astype(BF16)
        blocks.append(jnp.where(spot == here, jnp.ones((), BF16), jnp.zeros((), BF16)))
    return jnp.concatenate(blocks, 0)


def full(shape):
    return pl.BlockSpec(shape, lambda i: (0,) * len(shape))


def arr(shape, dtype):
    return jax.ShapeDtypeStruct(shape, dtype)


def call(kernel, name, grid, in_specs, out_specs, out_shape, scratch=(), mib=60, flops=10**6):
    return pl.pallas_call(
        kernel,
        name=name,
        grid=(grid,),
        in_specs=in_specs,
        out_specs=out_specs,
        out_shape=out_shape,
        scratch_shapes=list(scratch),
        compiler_params=pltpu.CompilerParams(vmem_limit_bytes=mib * 1024 * 1024),
        cost_estimate=pl.CostEstimate(flops=flops, bytes_accessed=10**5, transcendentals=0),
    )


SMEM = pl.BlockSpec(memory_space=pltpu.SMEM)


def prep_kernel(head_ref, tail_ref, table_ref, ints_ref,
                r_ref, q_ref, m_ref, pos_ref, rids_ref, th_ref, tt_ref, tn_ref, code_ref,
                high_ref, mid_ref, low_ref):
    table = table_ref[...]
    high = table.astype(BF16)
    rest = table - high.astype(F32)
    mid = rest.astype(BF16)
    low = (rest - mid.astype(F32)).astype(BF16)
    for ref, value in ((high_ref, high), (mid_ref, mid), (low_ref, low)):
        ref[:, pl.ds(REL_PAD - LANES, LANES)] = jnp.zeros((D, LANES), BF16)
        ref[:, pl.ds(0, RELS)] = value

    rids_ref[...] = ints_ref[:, :E_DEV]
    counts_row = ints_ref[:, AT_COUNTS:AT_COUNTS + N_OWN]
    counts = jnp.broadcast_to(counts_row, (N_OWN, N_OWN)).astype(F32)
    part = lax.broadcasted_iota(I32, (N_OWN, N_OWN), 0)
    other = lax.broadcasted_iota(I32, (N_OWN, N_OWN), 1)
    ends = jnp.sum(jnp.where(other <= part, counts, 0.0), 1, keepdims=True).astype(I32)
    own = jnp.sum(jnp.where(other == part, counts, 0.0), 1, keepdims=True).astype(I32)
    for out, at in ((th_ref, E_DEV), (tt_ref, 2 * E_DEV), (tn_ref, 3 * E_DEV)):
        slots = ints_ref[:, at:at + out.shape[1]]
        out[...] = slots + jnp.sum(jnp.where(slots >= ends, CAP - own, 0), 0, keepdims=True)

    place = lax.broadcasted_iota(I32, (U_CAP, N_OWN), 0)
    lane = (place & (CAP - 1)).astype(F32)
    owner = lax.broadcasted_iota(I32, (U_CAP, N_OWN), 1)
    counts_all = jnp.broadcast_to(counts_row, (U_CAP, N_OWN)).astype(F32)
    start = jnp.sum(jnp.where(owner < (place >> 4), counts_all, 0.0), 1, keepdims=True)
    count = jnp.sum(jnp.where(owner == (place >> 4), counts_all, 0.0), 1, keepdims=True)
    spot = (start + lane[:, :1]).astype(I32)
    column = lax.broadcasted_iota(I32, (U_CAP, U_CAP), 1)
    uid = ints_ref[:, AT_UID:AT_UID + U_CAP].astype(F32)
    picked = jnp.sum(jnp.where(column == spot, uid, 0.0), 1, keepdims=True)
    picked = jnp.where(lane[:, :1] < count, picked, float(ENT_DEV)).astype(I32)
    lanes = lax.broadcasted_iota(I32, (U_CAP, LANES), 1)
    code = jnp.where(lanes == USED, picked >> 5, jnp.where(lanes == USED + 1, picked & 31, 0))
    code_ref[...] = code.astype(F32)

    hit = one_hot(rids_ref[...], REL_PAD)
    rel = dot(high_ref[...], hit) + dot(mid_ref[...], hit) + dot(low_ref[...], hit)
    r_ref[...] = rel
    head = head_ref[...].astype(F32)
    tail = tail_ref[...].astype(F32)
    hr, hi, tr, ti, rr, ri = head[:HALF], head[HALF:], tail[:HALF], tail[HALF:], rel[:HALF], rel[HALF:]
    query = jnp.concatenate([hr * rr - hi * ri, hr * ri + hi * rr], 0).astype(BF16)
    mirror = jnp.concatenate([rr * tr + ri * ti, rr * ti - ri * tr], 0).astype(BF16)
    q_ref[...] = query
    m_ref[...] = mirror
    pos_t = jnp.sum(query.astype(F32) * tail, 0, keepdims=True)
    pos_h = jnp.sum(mirror.astype(F32) * head, 0, keepdims=True)
    side = lax.broadcasted_iota(I32, (8, E_DEV), 0)
    pos_ref[...] = jnp.where(side == 0, pos_t, pos_h)


def prep(heads, tails, table, ints):
    cols = lambda dt: arr((D, E_DEV), dt)
    return call(
        prep_kernel, "prep", 1,
        [full((D, E_DEV)), full((D, E_DEV)), full((D, RELS)), full((1, INTS))],
        [full((D, E_DEV))] * 3 + [full((8, E_DEV))] + [full((1, E_DEV))] * 3 + [full((1, NEG_DEV)), full((U_CAP, LANES))],
        [cols(F32), cols(BF16), cols(BF16), arr((8, E_DEV), F32),
         arr((1, E_DEV), I32), arr((1, E_DEV), I32), arr((1, E_DEV), I32), arr((1, NEG_DEV), I32), arr((U_CAP, LANES), F32)],
        [pltpu.VMEM((D, REL_PAD), BF16)] * 3,
        mib=24,
    )(heads, tails, table, ints)


def edge_kernel(core_ref, n0_ref, n1_ref, n2_ref, n3_ref, head_ref, tail_ref, r_ref, q_ref, m_ref, pos_ref, rid_ref,
                own_ref, g1_ref, g2_ref, g3_ref, rows_ref, mine_ref, other_ref, neg_ref, turned_ref):
    turn = eye(NEG_DEV)
    for k, ref in enumerate((n0_ref, n1_ref, n2_ref, n3_ref)):
        value = ref[...]
        neg_ref[:, pl.ds(k * NEG_DEV, NEG_DEV)] = value
        turned_ref[pl.ds(k * NEG_DEV, NEG_DEV), :] = dot_nt(turn, value).astype(BF16)

    head = head_ref[...].astype(F32)
    tail = tail_ref[...].astype(F32)
    firsts = []
    grads = []
    terms = []
    for side, (query_ref, positives) in enumerate(((q_ref, tail), (m_ref, head))):
        positive = pos_ref[pl.ds(side, 1), :]
        scores = dot(turned_ref[...], query_ref[...])
        top = jnp.maximum(positive, jnp.max(scores, 0, keepdims=True))
        weight = jnp.exp(scores - top)
        pos_weight = jnp.exp(positive - top)
        total = pos_weight + jnp.sum(weight, 0, keepdims=True)
        first = pos_weight / total - 1.0
        probs = (weight * (1.0 / total)).astype(BF16)
        terms.append(dot_nt(query_ref[...], probs))
        grads.append(first * positives + dot(neg_ref[...], probs))
        firsts.append(first)
    term = terms[0] + terms[1]
    own_ref[...] = term[:, :NEG_DEV]
    for k, ref in enumerate((g1_ref, g2_ref, g3_ref)):
        ref[...] = term[:, (k + 1) * NEG_DEV:(k + 2) * NEG_DEV].astype(BF16)

    rel = r_ref[...]
    dq, dm = grads
    hr, hi, tr, ti, rr, ri = head[:HALF], head[HALF:], tail[:HALF], tail[HALF:], rel[:HALF], rel[HALF:]
    qr, qi, mr, mi = dq[:HALF], dq[HALF:], dm[:HALF], dm[HALF:]
    d_rel = jnp.concatenate([(hr * qr + hi * qi) + (tr * mr + ti * mi), (hr * qi - hi * qr) + (ti * mr - tr * mi)], 0)
    ids = rid_ref[...] - REL_HALF * core_ref[0]
    ids = jnp.where(ids < 0, ids + REL_PAD, ids)
    hit = one_hot(ids, REL_PAD)
    high, low = split2(d_rel)
    both = jnp.concatenate([high, low], 0)
    for ref, at in ((other_ref, REL_HALF), (mine_ref, 0)):
        term = dot_nt(both, hit[at:at + REL_HALF])
        ref[...] = term[:D] + term[D:]

    d_head = firsts[1] * m_ref[...].astype(F32) + jnp.concatenate([rr * qr + ri * qi, rr * qi - ri * qr], 0)
    d_tail = firsts[0] * q_ref[...].astype(F32) + jnp.concatenate([rr * mr - ri * mi, rr * mi + ri * mr], 0)
    for k, value in enumerate((d_head, d_tail)):
        high, low = split2(value)
        rows_ref[:, pl.ds(k * E_DEV, E_DEV)] = high
        rows_ref[:, pl.ds((k + 2) * E_DEV, E_DEV)] = low


def edge(core, negs, h, t, r, q, m, pos, rid):
    part = (D, NEG_DEV)
    cols = (D, E_DEV)
    half = (D, REL_HALF)
    return call(
        edge_kernel, "edge", 1,
        [SMEM] + [full(part)] * 4 + [full(cols)] * 5 + [full((8, E_DEV)), full((1, E_DEV))],
        [full(part)] * 4 + [full((D, 4 * E_DEV))] + [full(half)] * 2,
        [arr(part, F32)] + [arr(part, BF16)] * 3 + [arr((D, 4 * E_DEV), BF16)] + [arr(half, F32)] * 2,
        [pltpu.VMEM((D, NEG), BF16), pltpu.VMEM((NEG, D), BF16)],
        flops=10**10, mib=36,
    )(core, *negs, h, t, r, q, m, pos, rid)


def slot_kernel(target_h_ref, target_t_ref, rows_ref, code_ref, out_ref):
    hit_h = one_hot(target_h_ref[...], U_CAP)
    hit_t = one_hot(target_t_ref[...], U_CAP)
    parts = [rows_ref[:, pl.ds(k * E_DEV, E_DEV)] for k in range(4)]
    total = (dot_nt(hit_h, parts[0]) + dot_nt(hit_h, parts[2])) + (dot_nt(hit_t, parts[1]) + dot_nt(hit_t, parts[3]))
    code = code_ref[:, USED:]
    for k in range(N_GRP):
        out_ref[k] = jnp.concatenate([total[:, k * USED:(k + 1) * USED], code], 1)


def slot(th, tt, rows, code):
    shape = (N_GRP, U_CAP, LANES)
    return call(
        slot_kernel, "slot", 1,
        [full((1, E_DEV))] * 2 + [full((D, 4 * E_DEV)), full((U_CAP, LANES))],
        full(shape), arr(shape, F32),
        flops=8 * 10**9, mib=24,
    )(th, tt, rows, code)


def pack_kernel(target_ref, own_ref, g1_ref, g2_ref, g3_ref, part_ref, out_ref):
    rows = own_ref[...] + g1_ref[...].astype(F32) + g2_ref[...].astype(F32) + g3_ref[...].astype(F32)
    hit = one_hot(target_ref[...], U_CAP)
    rest = jnp.zeros((LANES - USED, NEG_DEV), F32)
    for k in range(N_GRP):
        high, low = split2(jnp.concatenate([rows[k * USED:(k + 1) * USED], rest], 0))
        out_ref[k] = (part_ref[k] + (dot_nt(hit, high) + dot_nt(hit, low))).astype(BF16)


def pack(tn, own, g1, g2, g3, part):
    shape = (N_GRP, U_CAP, LANES)
    return call(
        pack_kernel, "pack", 1,
        [full((1, NEG_DEV))] + [full((D, NEG_DEV))] * 4 + [full(shape)],
        full(shape), arr(shape, BF16),
        flops=3 * 10**9, mib=16,
    )(tn, own, g1, g2, g3, part)


def partition_kernel(rows_ref, out_ref, acc_ref):
    step = pl.program_id(0)
    rows = rows_ref[...]
    lane = lax.broadcasted_iota(I32, (8, LANES), 1)
    weight = jnp.where(lane == USED, 32.0, jnp.where(lane == USED + 1, 1.0, 0.0)).astype(BF16)
    ids = dot_nt(weight, rows)[:1].astype(I32)
    group = jnp.broadcast_to(rows[:, USED:USED + 1], rows.shape)
    none = jnp.zeros((), BF16)
    lower = jnp.where(group < 16, rows, none)
    upper = jnp.where(group < 32, rows, none) - lower
    both = dot(one_hot(ids & (ENT_DEV // 2 - 1), ENT_DEV // 2), jnp.concatenate([lower, upper], 1))
    term = jnp.concatenate([both[:, :LANES], both[:, LANES:]], 0)

    @pl.when(step == 0)
    def _():
        acc_ref[...] = term

    @pl.when(step > 0)
    def _():
        acc_ref[...] += term

    @pl.when(step == pl.num_programs(0) - 1)
    def _():
        out_ref[...] = acc_ref[...].T[:USED]


def partition(rows):
    block = rows.shape[0]
    return call(
        partition_kernel, "partition", rows.shape[0] // block,
        [pl.BlockSpec((block, LANES), lambda i: (i, 0))],
        full((USED, ENT_DEV)),
        arr((USED, ENT_DEV), F32),
        [pltpu.VMEM((ENT_DEV, LANES), F32)],
        mib=32,
    )(rows)


def rel_chip_kernel(mine_ref, other_ref, out_ref):
    for k in range(REL_TILES):
        at = pl.ds(k * LANES, LANES)
        out_ref[pl.ds(k * D, D), :] = (mine_ref[:, at] + other_ref[:, at]).astype(BF16)
    rest = N_XY * REL_PART - REL_TILES * D
    out_ref[pl.ds(REL_TILES * D, rest), :] = jnp.zeros((rest, LANES), BF16)


def rel_chip(mine, other):
    shape = (N_XY * REL_PART, LANES)
    return call(rel_chip_kernel, "rel_chip", 1, [full((D, REL_HALF))] * 2, full(shape), arr(shape, BF16), mib=12)(mine, other)


def rel_xy_kernel(in_ref, out_ref):
    out_ref[...] = jnp.sum(in_ref[...].astype(F32), 0).astype(BF16)


def rel_xy(parts):
    shape = (REL_PART, LANES)
    return call(rel_xy_kernel, "rel_xy", 1, [full((N_XY,) + shape)], full(shape), arr(shape, BF16), mib=12)(parts)


def chip_pair_kernel(core_ref, mine_ref, other_ref, out_ref):
    at = pl.multiple_of(core_ref[0] * REL_PART, REL_PART)
    out_ref[pl.ds(at, REL_PART), :] = mine_ref[...]
    out_ref[pl.ds(REL_PART - at, REL_PART), :] = other_ref[...]


def chip_pair(core, mine, other):
    shape = (REL_PART, LANES)
    out = (2 * REL_PART, LANES)
    return call(chip_pair_kernel, "chip_pair", 1, [SMEM] + [full(shape)] * 2, full(out), arr(out, BF16), mib=12)(core, mine, other)


def split_pair_kernel(core_ref, b1_ref, b2_ref, b3_ref, far_ref, mine_ref, other_ref):
    at = pl.multiple_of(core_ref[0] * REL_PART, REL_PART)
    for k, ref in enumerate((b1_ref, b2_ref, b3_ref)):
        mine_ref[pl.ds(k * REL_PART, REL_PART), :] = ref[pl.ds(at, REL_PART), :]
        other_ref[pl.ds(k * REL_PART, REL_PART), :] = ref[pl.ds(REL_PART - at, REL_PART), :]
    mine_ref[pl.ds(3 * REL_PART, REL_PART), :] = far_ref[...]


def split_pair(core, blocks, far):
    rows = (4 * REL_PART, LANES), (3 * REL_PART, LANES)
    return call(
        split_pair_kernel, "split_pair", 1, [SMEM] + [full((2 * REL_PART, LANES))] * 3 + [full((REL_PART, LANES))],
        [full(shape) for shape in rows], [arr(shape, BF16) for shape in rows], mib=12, flops=3 * 10**10
    )(core, *blocks, far)


def rel_z_kernel(core_ref, own_ref, mine_ref, other_ref, out_ref):
    value = lambda ref, k: ref[pl.ds(k * REL_PART, REL_PART), :].astype(F32)
    ahead = [value(mine_ref, k) for k in range(3)]
    behind = [value(other_ref, k) for k in range(3)]
    first = core_ref[0] == 0
    back = [own_ref[...].astype(F32)] + [jnp.where(first, a, b) for a, b in zip(ahead, behind)]
    back += [value(mine_ref, 3)] + [jnp.where(first, b, a) for a, b in zip(ahead[::-1], behind[::-1])]
    values = back
    while len(values) > 1:
        half = len(values) // 2
        values = [values[k] + values[k + half] for k in range(half)]
    out_ref[...] = values[0].astype(BF16)


def rel_z(core, own, mine, other):
    shape = (REL_PART, LANES)
    return call(
        rel_z_kernel, "rel_z", 1, [SMEM, full(shape), full((4 * REL_PART, LANES)), full((3 * REL_PART, LANES))], full(shape),
        arr(shape, BF16), mib=12,
    )(core, own, mine, other)


def place_kernel(me_ref, *refs):
    out_ref = refs[-1]
    rows = refs[0].shape[0]
    for k, ref in enumerate(refs[:-1]):
        at = pl.multiple_of(((me_ref[0] - k) & (N_GRP - 1)) * rows, rows)
        out_ref[pl.ds(at, rows), :] = ref[...]


def place(me, blocks, name):
    rows = blocks[0].shape[0]
    shape = (rows * N_GRP, LANES)
    return call(
        place_kernel, name, 1, [SMEM] + [full((rows, LANES))] * N_GRP, full(shape), arr(shape, BF16), mib=12
    )(me, *blocks)


def table_kernel(core_ref, mine_ref, other_ref, out_ref):
    for half, ref in enumerate((mine_ref, other_ref)):
        for place in range(2):
            @pl.when((core_ref[0] == half) == (place == 0))
            def _(ref=ref, place=place):
                for k in range(REL_TILES):
                    at = place * REL_HALF + k * LANES
                    width = min(LANES, RELS - at)
                    out_ref[:, pl.ds(at, width)] = ref[pl.ds(k * D, D), :].astype(F32)[:, :width]


def table(core, mine, other):
    return call(
        table_kernel, "table", 1, [SMEM] + [full((N_XY * REL_PART, LANES))] * 2, full((D, RELS)), arr((D, RELS), F32), mib=20
    )(core, mine, other)


def shift(value, axis, k, size=N_GRP):
    return lax.ppermute(value, axis, [(i, (i + k) % size) for i in range(size)])


def pair(value):
    return lax.ppermute(value, "c", [(0, 1), (1, 0)])


def shift_zc(value, ahead):
    pairs = [(2 * z + c, 2 * ((z + ahead[c]) % 8) + c) for z in range(8) for c in range(2)]
    return lax.ppermute(value, ("z", "c"), pairs)


def around(value, axis):
    return [value] + [shift(value, axis, k) for k in (1, 2, 3)]


def shards(head_rows, tail_rows, rel_ids, neg_rows, rel_table, owner_counts, unique_ids, head_slot, tail_slot, negative_slot):
    core = lax.axis_index("c").astype(I32).reshape(1)
    x = lax.axis_index("x").astype(I32).reshape(1)
    y = lax.axis_index("y").astype(I32).reshape(1)
    heads, tails = head_rows.T, tail_rows.T
    negs = around(neg_rows.T, "x")
    ints = jnp.concatenate([
        rel_ids, head_slot, tail_slot, negative_slot, unique_ids[0], owner_counts[0],
        jnp.zeros((INTS - AT_COUNTS - N_OWN,), I32)]).reshape(1, INTS)
    r, q, m, pos, rid, th, tt, tn, code = prep(heads, tails, rel_table.T, ints)
    own, g1, g2, g3, rows, mine, other = edge(core, negs, heads, tails, r, q, m, pos, rid)
    back = [shift(g, "x", N_GRP - k) for k, g in ((1, g1), (2, g2), (3, g3))]
    other = pair(other)
    chip = rel_chip(mine, other).reshape(N_XY, REL_PART, LANES)
    part = slot(th, tt, rows, code)
    chip = lax.all_to_all(chip, ("x", "y"), 0, 0, tiled=True)
    packed = pack(tn, own, *back, part)
    chip, packed = lax.optimization_barrier((chip, packed))
    piece = rel_xy(chip)
    piece, packed = lax.optimization_barrier((piece, packed))
    both = chip_pair(core, piece, pair(piece))
    mine, other = split_pair(core, [shift_zc(both, ahead) for ahead in ((1, 7), (2, 6), (3, 5))], shift(piece, "z", 4, 8))
    piece = rel_z(core, piece, mine, pair(other))
    received = lax.all_to_all(packed.reshape(N_GRP * N_OWN, CAP, LANES), ALL, 0, 0, tiled=True)
    quarter = place(y, around(piece, "y"), "place_y")
    half = place(x, around(quarter, "x"), "place_x")
    rel_grad = table(core, half, pair(half))
    entity_grad = partition(received.reshape(-1, LANES))
    return entity_grad.T, rel_grad.T


def solution(mesh):
    split = Mesh(mesh.devices.reshape(N_GRP, 4, 8, 2), ALL)
    edges = P(ALL)
    rows = P(ALL, None)
    in_specs = (rows, rows, edges, rows, P(), rows, rows, edges, edges, edges)
    out_specs = (P(("y", "z", "c"), "x"), P())
    return jax.shard_map(shards, mesh=split, in_specs=in_specs, out_specs=out_specs, check_vma=False)
```
